32 devices in a mesh: grp: 4 (over y, core), row: 8 (over z, x).
Axes of the slice: x: 2, y: 2, z: 4, core: 2. Of those that a mesh axis runs over, the one named last changes fastest.
Arguments:
- features: bfloat16 [65536, 256], P(('grp', 'row')), may hold values from -6 to 6
- cotangent: bfloat16 [65536, 256], P(('grp', 'row')), may hold values from -6 to 6
- self_weight: bfloat16 [256, 256], replicated, may hold values from -0.375 to 0.375
- neighbor_weight: bfloat16 [256, 256], replicated, may hold values from -0.375 to 0.375
- tile_values: bfloat16 [32, 64, 128, 128], P(('grp', 'row')), may hold values from 0 to 1
- tile_index: int32 [32, 64, 2], P(('grp', 'row')), may hold values from 0 to 15
- hub_adjacency: bfloat16 [65536, 1024], P(('grp', 'row')), may hold values from 0 to 1
- hub_owner: int32 [4, 8], P('grp'), may hold values from 0 to 7
- send_rows: int32 [32, 4, 64], P(('grp', 'row')), may hold values from 0 to 2047
- cut_adjacency: bfloat16 [65536, 256], P(('grp', 'row')), may hold values from 0 to 1
- degrees: int32 [65536], P(('grp', 'row')), may hold values from 896 to 1791
Outputs:
- hidden: bfloat16 [65536, 256], P(('grp', 'row'))
- grad_features: bfloat16 [65536, 256], P(('grp', 'row'))
- grad_self: float32 [256, 256], replicated
- grad_neighbor: float32 [256, 256], replicated
The draws below stay inside these ranges and needn't reach their ends.
Inputs may be any that keep to these rules, and one draw needn't show every extreme that they name: `send_rows`: rows may repeat.
All inputs are finite; a program needn't handle non-finite values.
Results may differ from the reference program's by a relative error of at most 0.014.
Values may be sent and summed in bfloat16 or wider, within the bound.
No kernel may reach another device: no remote copies, remote signals or barrier semaphores. Data moves between devices by JAX's collectives and lax.ppermute only.
A program may use at most 128 MiB of HBM per device.

```python
import jax
import jax.numpy as jnp
from jax import lax

WIDTH = 256
TILE = 128
TILES_DEV = 16
HUB = 128
SECTIONS = 8
CUT = 64
TILES = 64
NODE_DEV = 2048
NODES = 65536
NEIGHBORS = 1792
N_GRP = 4
N_ROW = 8


def touch_ends(entries, own_key, low, top_value):
    longest = entries.shape.index(max(entries.shape))
    spots = []
    for shift in (0, 1):
        where = [jax.random.randint(jax.random.fold_in(own_key, axis), (), 0, length) for axis, length in enumerate(entries.shape)]
        where[longest] = (where[longest] + shift) % entries.shape[longest]
        spots.append(tuple(where))
    return entries.at[spots[0]].set(low).at[spots[1]].set(top_value)


def block_levels(own_key, extent, cuts, low, high):
    loudness, own = 1.0, jax.random.fold_in(own_key, 6)
    for dim, shards_of in cuts:
        steps = jnp.exp(jax.random.uniform(jax.random.fold_in(own, dim), (shards_of,), jnp.float32, low / len(cuts), high / len(cuts)))
        loudness = loudness * jnp.repeat(steps, extent[dim] // shards_of).reshape([-1 if axis == dim else 1 for axis in range(len(extent))])
    return loudness


def scatter_about(key, shape, spread, most, cuts=(), kind=jnp.bfloat16):
    drawn = jax.random.normal(key, shape, jnp.float32) * spread
    if len(cuts) > 0:
        drawn = block_levels(key, shape, cuts, -0.22, 0.18) * drawn
    return jnp.clip(drawn, min=-most, max=most).astype(kind)


def setup_inputs(seed: int = 0) -> dict:
    key_of = jax.random.split(jax.random.key(seed), 12)
    return {
        "features": scatter_about(key_of[0], (NODES, WIDTH), 1.0, 6.0, ((0, 32),)),
        "cotangent": scatter_about(key_of[1], (NODES, WIDTH), 1.0, 6.0, ((0, 32),)),
        "self_weight": scatter_about(key_of[2], (WIDTH, WIDTH), WIDTH ** -0.5, 0.375),
        "neighbor_weight": scatter_about(key_of[3], (WIDTH, WIDTH), WIDTH ** -0.5, 0.375),
        "tile_values": jnp.clip(1.0 * jax.random.uniform(key_of[4], (N_GRP * N_ROW, TILES, TILE, TILE), jnp.float32) ** block_levels(key_of[4], (N_GRP * N_ROW, TILES, TILE, TILE), ((0, 32),), -0.2, 0.2), 0.0, 1.0).astype(jnp.bfloat16),
        "tile_index": touch_ends(jax.random.randint(key_of[5], (N_GRP * N_ROW, TILES, 2), 0, TILES_DEV), jax.random.fold_in(key_of[5], 1), 0, TILES_DEV - 1).astype(jnp.int32),
        "hub_adjacency": jnp.clip(1.0 * jax.random.uniform(key_of[6], (NODES, SECTIONS * HUB), jnp.float32) ** block_levels(key_of[6], (NODES, SECTIONS * HUB), ((0, 32),), -0.2, 0.2), 0.0, 1.0).astype(jnp.bfloat16),
        "hub_owner": touch_ends(jax.random.randint(key_of[7], (N_GRP, SECTIONS), 0, N_ROW), jax.random.fold_in(key_of[7], 1), 0, N_ROW - 1).astype(jnp.int32),
        "send_rows": touch_ends(jax.random.randint(key_of[8], (N_GRP * N_ROW, N_GRP, CUT), 0, NODE_DEV), jax.random.fold_in(key_of[8], 1), 0, NODE_DEV - 1).astype(jnp.int32),
        "cut_adjacency": jnp.clip(1.0 * jax.random.uniform(key_of[9], (NODES, N_GRP * CUT), jnp.float32) ** block_levels(key_of[9], (NODES, N_GRP * CUT), ((0, 32),), -0.2, 0.2), 0.0, 1.0).astype(jnp.bfloat16),
        "degrees": touch_ends(jax.random.randint(key_of[10], (NODES,), NEIGHBORS // 2, NEIGHBORS), jax.random.fold_in(key_of[10], 1), NEIGHBORS // 2, NEIGHBORS - 1).astype(jnp.int32),
    }


def device_pass(items, self_weight, neighbor_weight):
    features, cotangent, values, index, hub_rows, panels, cut_rows, arrived, degree = items
    tile_total = features.shape[0] // TILE
    width = features.shape[1]
    blocks = features.reshape(tile_total, TILE, width)
    row_select = (index[:, 0][None, :] == jnp.arange(tile_total)[:, None]).astype(jnp.float32)
    col_select = (index[:, 1][None, :] == jnp.arange(tile_total)[:, None]).astype(jnp.float32)
    picked = blocks[index[:, 1]]
    product = jnp.einsum('lab,lbf->laf', values.astype(jnp.float32), picked.astype(jnp.float32), precision=lax.Precision.HIGHEST)
    local_sum = jnp.einsum('nl,laf->naf', row_select, product, precision=lax.Precision.HIGHEST).reshape(-1, width)
    hub_sum = jnp.dot(hub_rows, panels, preferred_element_type=jnp.float32)
    cut_sum = jnp.dot(cut_rows, arrived, preferred_element_type=jnp.float32)
    scaling = lax.rsqrt(degree.astype(jnp.float32))[:, None]
    aggregated = ((local_sum + hub_sum + cut_sum) * scaling).astype(jnp.bfloat16)
    before = jnp.dot(features, self_weight, preferred_element_type=jnp.float32) + jnp.dot(aggregated, neighbor_weight, preferred_element_type=jnp.float32)
    activated, pullback = jax.vjp(jax.nn.gelu, before)
    hidden = activated.astype(jnp.bfloat16)
    grad_before = pullback(cotangent.astype(before.dtype))[0].astype(jnp.bfloat16)
    rows_dims = (((0,), (0,)), ((), ()))
    cols_dims = (((1,), (1,)), ((), ()))
    self_part = lax.dot_general(features, grad_before, rows_dims, preferred_element_type=jnp.float32)
    neighbor_part = lax.dot_general(aggregated, grad_before, rows_dims, preferred_element_type=jnp.float32)
    grad_aggregate = (lax.dot_general(grad_before, neighbor_weight, cols_dims, preferred_element_type=jnp.float32) * scaling).astype(jnp.bfloat16)
    grad_part = lax.dot_general(grad_before, self_weight, cols_dims, preferred_element_type=jnp.float32)
    agg_blocks = grad_aggregate.reshape(tile_total, TILE, width)[index[:, 0]]
    returned = jnp.einsum('lab,laf->lbf', values.astype(jnp.float32), agg_blocks.astype(jnp.float32), precision=lax.Precision.HIGHEST)
    grad_part = grad_part + jnp.einsum('nl,lbf->nbf', col_select, returned, precision=lax.Precision.HIGHEST).reshape(-1, width)
    hub_terms = lax.dot_general(hub_rows, grad_aggregate, rows_dims, preferred_element_type=jnp.float32)
    back_rows = lax.dot_general(cut_rows, grad_aggregate, rows_dims, preferred_element_type=jnp.float32).astype(jnp.bfloat16)
    return (hidden, grad_part, self_part, neighbor_part, hub_terms, back_rows)

def scatter_back(items):
    returned, rows = items
    table = (rows[None, :] == jnp.arange(NODE_DEV)[:, None]).astype(jnp.bfloat16)
    return jnp.dot(table, returned, preferred_element_type=jnp.float32)

def reference(features, cotangent, self_weight, neighbor_weight, tile_values, tile_index, hub_adjacency, hub_owner, send_rows, cut_adjacency, degrees):
    groups = N_GRP
    rows_axis = N_ROW
    blocks_all = groups * rows_axis
    width = WIDTH
    block_feats = features.reshape(blocks_all, NODE_DEV, width)
    block_cots = cotangent.reshape(blocks_all, NODE_DEV, width)
    block_hubs = hub_adjacency.reshape(blocks_all, NODE_DEV, SECTIONS * HUB)
    block_cuts = cut_adjacency.reshape(blocks_all, NODE_DEV, groups * CUT)
    block_degs = degrees.reshape(blocks_all, NODE_DEV)
    heads = block_feats[:, :HUB].reshape(groups, rows_axis, HUB, width)
    panels = heads[jnp.arange(groups)[:, None], hub_owner]
    panels = jnp.broadcast_to(panels.reshape(groups, 1, SECTIONS * HUB, width), (groups, rows_axis, SECTIONS * HUB, width)).reshape(blocks_all, SECTIONS * HUB, width)
    outgoing = jax.vmap(lambda block, rows: block[rows])(block_feats, send_rows)
    arrived = outgoing.reshape(groups, rows_axis, groups, CUT, width).transpose(2, 1, 0, 3, 4).reshape(blocks_all, groups * CUT, width)
    items = (block_feats, block_cots, tile_values, tile_index, block_hubs, panels, block_cuts, arrived, block_degs)
    hidden, grad_part, self_parts, neighbor_parts, hub_terms, back_rows = lax.map(lambda item: device_pass(item, self_weight, neighbor_weight), items)
    grad_self = lax.optimization_barrier(jnp.sum(self_parts, axis=0))
    grad_neighbor = lax.optimization_barrier(jnp.sum(neighbor_parts, axis=0))
    hub_total = hub_terms.reshape(groups, rows_axis, SECTIONS, HUB, width).sum(axis=1)
    owned = (hub_owner[:, :, None] == jnp.arange(rows_axis)[None, None, :]).astype(hub_total.dtype)
    hub_grad = jnp.einsum('gsr,gshf->grhf', owned, hub_total, precision=lax.Precision.HIGHEST).reshape(blocks_all, HUB, width)
    returned = back_rows.reshape(groups, rows_axis, groups, CUT, width).transpose(2, 1, 0, 3, 4).reshape(blocks_all, groups * CUT, width)
    cut_grad = lax.map(scatter_back, (returned, send_rows.reshape(blocks_all, groups * CUT)))
    total = grad_part + cut_grad
    total = total.at[:, :HUB].add(hub_grad)
    return (hidden.reshape(NODES, width), total.astype(jnp.bfloat16).reshape(NODES, width), grad_self, grad_neighbor)
```

```python
import jax
import jax.numpy as jnp
from jax import lax
from jax.experimental import pallas as pl
from jax.experimental.pallas import tpu as pltpu
from jax.sharding import PartitionSpec as P

TILE = 128
HUB = 128
CHUNK = 256
TILE_STEP = 8
VMEM_LIMIT = 48 * 2**20
ROWS = (((0,), (0,)), ((), ()))
COLS = (((1,), (1,)), ((), ()))
F32 = jnp.float32
BF16 = jnp.bfloat16


def params():
    return pltpu.CompilerParams(
        dimension_semantics=("arbitrary",), vmem_limit_bytes=VMEM_LIMIT
    )


def cost(flops, bytes_accessed):
    return pl.CostEstimate(flops=flops, bytes_accessed=bytes_accessed, transcendentals=0)


def dot(a, b, dims=(((1,), (0,)), ((), ()))):
    return lax.dot_general(a, b, dims, preferred_element_type=F32)


def whole(shape):
    return pl.BlockSpec(shape, lambda i, *_: (0,) * len(shape))


def rows_of(step, width):
    return pl.BlockSpec((step, width), lambda i, *_: (i, 0))


def pick_kernel(rows_ref, features_ref, out_ref):
    count = features_ref.shape[0]
    where = lax.broadcasted_iota(jnp.int32, (rows_ref.shape[0], count), 1)
    table = jnp.where(where == rows_ref[...], 1.0, 0.0).astype(BF16)
    out_ref[...] = dot(table, features_ref[...]).astype(BF16)


def pick_rows(rows, features):
    picks = rows.shape[0]
    count, width = features.shape
    step = 128
    return pl.pallas_call(
        pick_kernel,
        grid=(picks // step,),
        in_specs=[rows_of(step, 1), whole((count, width))],
        out_specs=rows_of(step, width),
        out_shape=jax.ShapeDtypeStruct((picks, width), BF16),
        compiler_params=params(),
        cost_estimate=cost(2 * picks * count * width, 2 * count * width),
        name="pick_rows",
    )(rows, features)


def local_kernel(index_ref, values_ref, features_ref, out_ref):
    step = pl.program_id(0)

    @pl.when(step == 0)
    def _():
        out_ref[...] = jnp.zeros_like(out_ref)

    for t in range(TILE_STEP):
        at = step * TILE_STEP + t
        row = pl.ds(pl.multiple_of(index_ref[at, 0] * TILE, TILE), TILE)
        col = pl.ds(pl.multiple_of(index_ref[at, 1] * TILE, TILE), TILE)
        out_ref[row, :] += dot(values_ref[t], features_ref[col, :])


def local_forward(index, values, features):
    tiles = values.shape[0]
    count, width = features.shape
    return pl.pallas_call(
        local_kernel,
        grid_spec=pltpu.PrefetchScalarGridSpec(
            num_scalar_prefetch=1,
            grid=(tiles // TILE_STEP,),
            in_specs=[
                pl.BlockSpec((TILE_STEP, TILE, TILE), lambda i, *_: (i, 0, 0)),
                whole((count, width)),
            ],
            out_specs=whole((count, width)),
        ),
        out_shape=jax.ShapeDtypeStruct((count, width), F32),
        compiler_params=params(),
        cost_estimate=cost(2 * tiles * TILE * TILE * width, 2 * values.size + 6 * features.size),
        name="local_forward",
    )(index, values, features)


def forward_kernel(
    owner_ref,
    hub_ref,
    heads_ref,
    cut_ref,
    arrived_ref,
    local_ref,
    scale_ref,
    features_ref,
    cotangent_ref,
    self_ref,
    neighbor_ref,
    hidden_ref,
    grad_ref,
    weights_ref,
    panels,
    total,
):
    step = pl.program_id(0)
    sections = panels.shape[0] // HUB
    width = features_ref.shape[1]

    @pl.when(step == 0)
    def _():
        total[...] = jnp.zeros_like(total)
        for s in range(sections):
            panels[s * HUB : (s + 1) * HUB, :] = heads_ref[owner_ref[s]]

    summed = dot(hub_ref[...], panels[...]) + dot(cut_ref[...], arrived_ref[...]) + local_ref[...]
    aggregated = (summed * scale_ref[...]).astype(BF16)
    features = features_ref[...]
    before = dot(features, self_ref[...]) + dot(aggregated, neighbor_ref[...])
    root = 0.7978845608028654
    square = before * before
    bend = jnp.tanh(root * before * (1.0 + 0.044715 * square))
    half = 0.5 + 0.5 * bend
    hidden_ref[...] = (before * half).astype(BF16)
    slope = half + (0.5 * root) * before * (1.0 - bend * bend) * (1.0 + (3 * 0.044715) * square)
    grad = (cotangent_ref[...].astype(F32) * slope).astype(BF16)
    grad_ref[...] = grad
    total[:width, :] += dot(features, grad, ROWS)
    total[width:, :] += dot(aggregated, grad, ROWS)

    @pl.when(step == pl.num_programs(0) - 1)
    def _():
        weights_ref[...] = total[...].astype(BF16)


def forward(owners, hub, heads, cut, arrived, local, scale, features, cotangent, self_weight, neighbor_weight):
    count, width = features.shape
    sections = hub.shape[1] // HUB
    flops = 2 * count * width * (hub.shape[1] + cut.shape[1] + 4 * width)
    return pl.pallas_call(
        forward_kernel,
        grid_spec=pltpu.PrefetchScalarGridSpec(
            num_scalar_prefetch=1,
            grid=(count // CHUNK,),
            in_specs=[
                rows_of(CHUNK, hub.shape[1]),
                whole(heads.shape),
                rows_of(CHUNK, cut.shape[1]),
                whole(arrived.shape),
                rows_of(CHUNK, width),
                rows_of(CHUNK, 1),
                rows_of(CHUNK, width),
                rows_of(CHUNK, width),
                whole((width, width)),
                whole((width, width)),
            ],
            out_specs=[rows_of(CHUNK, width), rows_of(CHUNK, width), whole((2 * width, width))],
            scratch_shapes=[
                pltpu.VMEM((sections * HUB, width), BF16),
                pltpu.VMEM((2 * width, width), F32),
            ],
        ),
        out_shape=[
            jax.ShapeDtypeStruct((count, width), BF16),
            jax.ShapeDtypeStruct((count, width), BF16),
            jax.ShapeDtypeStruct((2 * width, width), BF16),
        ],
        compiler_params=params(),
        cost_estimate=cost(flops, 2 * hub.size + 2 * cut.size + 14 * features.size),
        name="forward",
    )(owners, hub, heads, cut, arrived, local, scale, features, cotangent, self_weight, neighbor_weight)


def backward_kernel(
    owner_ref, hub_ref, cut_ref, scale_ref, grad_ref, neighbor_ref, aggregate_ref, heads_ref, back_ref, hub_total, cut_total
):
    step = pl.program_id(0)
    sections = hub_ref.shape[1] // HUB

    @pl.when(step == 0)
    def _():
        hub_total[...] = jnp.zeros_like(hub_total)
        cut_total[...] = jnp.zeros_like(cut_total)

    aggregate = (dot(grad_ref[...], neighbor_ref[...], COLS) * scale_ref[...]).astype(BF16)
    aggregate_ref[...] = aggregate
    hub_total[...] += dot(hub_ref[...], aggregate, ROWS)
    cut_total[...] += dot(cut_ref[...], aggregate, ROWS)

    @pl.when(step == pl.num_programs(0) - 1)
    def _():
        back_ref[...] = cut_total[...].astype(BF16)
        for r in range(heads_ref.shape[0]):
            piece = jnp.zeros(heads_ref.shape[1:], F32)
            for s in range(sections):
                mine = jnp.where(owner_ref[s] == r, 1.0, 0.0).astype(F32)
                piece = piece + mine * hub_total[s * HUB : (s + 1) * HUB, :]
            heads_ref[r] = piece.astype(BF16)


def backward(owners, hub, cut, scale, grad, neighbor_weight, row_count):
    count, width = grad.shape
    flops = 2 * count * width * (hub.shape[1] + cut.shape[1] + width)
    return pl.pallas_call(
        backward_kernel,
        grid_spec=pltpu.PrefetchScalarGridSpec(
            num_scalar_prefetch=1,
            grid=(count // CHUNK,),
            in_specs=[
                rows_of(CHUNK, hub.shape[1]),
                rows_of(CHUNK, cut.shape[1]),
                rows_of(CHUNK, 1),
                rows_of(CHUNK, width),
                whole((width, width)),
            ],
            out_specs=[
                rows_of(CHUNK, width),
                whole((row_count, HUB, width)),
                whole((cut.shape[1], width)),
            ],
            scratch_shapes=[
                pltpu.VMEM((hub.shape[1], width), F32),
                pltpu.VMEM((cut.shape[1], width), F32),
            ],
        ),
        out_shape=[
            jax.ShapeDtypeStruct((count, width), BF16),
            jax.ShapeDtypeStruct((row_count, HUB, width), BF16),
            jax.ShapeDtypeStruct((cut.shape[1], width), BF16),
        ],
        compiler_params=params(),
        cost_estimate=cost(flops, 2 * hub.size + 2 * cut.size + 4 * grad.size),
        name="backward",
    )(owners, hub, cut, scale, grad, neighbor_weight)


def local_back_kernel(index_ref, values_ref, aggregate_ref, grad_ref, self_ref, out_ref):
    step = pl.program_id(0)

    @pl.when(step == 0)
    def _():
        out_ref[...] = dot(grad_ref[...], self_ref[...], COLS)

    for t in range(TILE_STEP):
        at = step * TILE_STEP + t
        row = pl.ds(pl.multiple_of(index_ref[at, 0] * TILE, TILE), TILE)
        col = pl.ds(pl.multiple_of(index_ref[at, 1] * TILE, TILE), TILE)
        out_ref[col, :] += dot(values_ref[t], aggregate_ref[row, :], ROWS)


def local_backward(index, values, aggregate, grad, self_weight):
    tiles = values.shape[0]
    count, width = grad.shape
    return pl.pallas_call(
        local_back_kernel,
        grid_spec=pltpu.PrefetchScalarGridSpec(
            num_scalar_prefetch=1,
            grid=(tiles // TILE_STEP,),
            in_specs=[
                pl.BlockSpec((TILE_STEP, TILE, TILE), lambda i, *_: (i, 0, 0)),
                whole((count, width)),
                whole((count, width)),
                whole((width, width)),
            ],
            out_specs=whole((count, width)),
        ),
        out_shape=jax.ShapeDtypeStruct((count, width), F32),
        compiler_params=params(),
        cost_estimate=cost(
            2 * tiles * TILE * TILE * width + 2 * count * width * width,
            2 * values.size + 8 * grad.size,
        ),
        name="local_backward",
    )(index, values, aggregate, grad, self_weight)


def finish_kernel(rows_ref, returned_ref, heads_ref, local_ref, out_ref):
    step = pl.program_id(0)
    picks = returned_ref.shape[0]
    where = lax.broadcasted_iota(jnp.int32, (CHUNK, picks), 0) + step * CHUNK
    table = jnp.where(where == rows_ref[...], 1.0, 0.0).astype(BF16)
    total = local_ref[...] + dot(table, returned_ref[...])
    out_ref[...] = total.astype(BF16)

    @pl.when(step == 0)
    def _():
        heads = jnp.sum(heads_ref[...].astype(F32), axis=0)
        out_ref[:HUB, :] = (total[:HUB, :] + heads).astype(BF16)


def finish(rows, returned, heads, local):
    count, width = local.shape
    picks = returned.shape[0]
    return pl.pallas_call(
        finish_kernel,
        grid=(count // CHUNK,),
        in_specs=[
            whole((1, picks)),
            whole((picks, width)),
            whole(heads.shape),
            rows_of(CHUNK, width),
        ],
        out_specs=rows_of(CHUNK, width),
        out_shape=jax.ShapeDtypeStruct((count, width), BF16),
        compiler_params=params(),
        cost_estimate=cost(2 * count * picks * width, 6 * local.size),
        name="finish",
    )(rows, returned, heads, local)


def on_device(
    features,
    cotangent,
    self_weight,
    neighbor_weight,
    tile_values,
    tile_index,
    hub_adjacency,
    hub_owner,
    send_rows,
    cut_adjacency,
    degrees,
):
    count, width = features.shape
    groups = lax.axis_size("grp")
    row_count = lax.axis_size("row")
    everyone = ("grp", "row")
    device_count = groups * row_count
    values = tile_values[0]
    index = tile_index[0]
    owners = hub_owner[0]
    rows = send_rows[0].reshape(-1)

    heads = jnp.broadcast_to(features[:HUB][None], (row_count, HUB, width))
    heads = lax.all_to_all(heads, "row", split_axis=0, concat_axis=0, tiled=True)
    outgoing = pick_rows(rows[:, None], features)
    arrived = lax.all_to_all(outgoing, "grp", split_axis=0, concat_axis=0, tiled=True)
    scale = lax.rsqrt(degrees.astype(F32))[:, None]
    local = local_forward(index, values, features)
    hidden, grad, weights = forward(
        owners, hub_adjacency, heads, cut_adjacency, arrived, local, scale,
        features, cotangent, self_weight, neighbor_weight,
    )
    parts = lax.all_to_all(weights, everyone, split_axis=0, concat_axis=0, tiled=True)
    aggregate, head_parts, back_rows = backward(
        owners, hub_adjacency, cut_adjacency, scale, grad, neighbor_weight, row_count
    )
    head_parts = lax.all_to_all(head_parts, "row", split_axis=0, concat_axis=0, tiled=True)
    returned = lax.all_to_all(back_rows, "grp", split_axis=0, concat_axis=0, tiled=True)
    local_grad = local_backward(index, values, aggregate, grad, self_weight)
    summed = jnp.sum(parts.reshape(device_count, -1, width).astype(F32), axis=0).astype(BF16)
    spread = jnp.broadcast_to(summed[None], (device_count, *summed.shape))
    spread = lax.all_to_all(spread, everyone, split_axis=0, concat_axis=0, tiled=True)
    weight_grads = spread.reshape(2 * width, width).astype(F32)
    grad_features = finish(rows[None, :], returned, head_parts, local_grad)
    return hidden, grad_features, weight_grads[:width], weight_grads[width:]


def solution(mesh):
    nodes = P(("grp", "row"), None)
    in_specs = (
        nodes,
        nodes,
        P(),
        P(),
        P(("grp", "row"), None, None, None),
        P(("grp", "row"), None, None),
        nodes,
        P("grp", None),
        P(("grp", "row"), None, None),
        nodes,
        P(("grp", "row")),
    )
    out_specs = (nodes, nodes, P(), P())
    return jax.shard_map(
        on_device, mesh=mesh, in_specs=in_specs, out_specs=out_specs, check_vma=False
    )
```

```python
import functools

import jax
import jax.numpy as jnp
from jax import lax
from jax.experimental import pallas as pl
from jax.experimental.pallas import tpu as pltpu
from jax.sharding import PartitionSpec as P

TILE = 128
HUB = 128
CHUNK = 256
TILE_STEP = 8
VMEM_LIMIT = 48 * 2**20
ROWS = (((0,), (0,)), ((), ()))
COLS = (((1,), (1,)), ((), ()))
F32 = jnp.float32
BF16 = jnp.bfloat16


def params():
    return pltpu.CompilerParams(
        dimension_semantics=("arbitrary",), vmem_limit_bytes=VMEM_LIMIT
    )


def cost(flops, bytes_accessed):
    return pl.CostEstimate(flops=flops, bytes_accessed=bytes_accessed, transcendentals=0)


def dot(a, b, dims=(((1,), (0,)), ((), ()))):
    return lax.dot_general(a, b, dims, preferred_element_type=F32)


def whole(shape):
    return pl.BlockSpec(shape, lambda i, *_: (0,) * len(shape))


def rows_of(step, width):
    return pl.BlockSpec((step, width), lambda i, *_: (i, 0))


def pick_kernel(place_ref, rows_ref, features_ref, own_ref, odd_ref, *rest):
    even_refs, picked = rest[:-1], rest[-1]
    count = features_ref.shape[0]
    lanes = rows_ref.shape[1]
    across = lax.broadcasted_iota(jnp.int32, (lanes, lanes), 0)
    along = lax.broadcasted_iota(jnp.int32, (lanes, lanes), 1)
    where = lax.broadcasted_iota(jnp.int32, (lanes, count), 1)
    for j in range(rows_ref.shape[0]):
        line = jnp.broadcast_to(rows_ref[j : j + 1, :].astype(F32), (lanes, lanes))
        column = jnp.sum(jnp.where(across == along, line, 0.0), axis=1, keepdims=True)
        table = jnp.where(where == column.astype(jnp.int32), 1.0, 0.0).astype(BF16)
        picked[j * lanes : (j + 1) * lanes, :] = dot(table, features_ref[...]).astype(BF16)
    cut = own_ref.shape[0]

    def piece(k):
        return picked[pl.ds(pl.multiple_of((place_ref[0] ^ k) * cut, cut), cut), :]

    own_ref[...] = piece(0)
    for j in range(odd_ref.shape[0]):
        odd_ref[j] = piece(2 * j + 1)
    for j, ref in enumerate(even_refs):
        ref[...] = piece(2 * j + 2)


def pick_rows(place, rows, features):
    groups, cut = rows.shape
    picks = groups * cut
    count, width = features.shape
    evens = groups // 2 - 1
    piece = jax.ShapeDtypeStruct((cut, width), BF16)
    out = pl.pallas_call(
        pick_kernel,
        grid_spec=pltpu.PrefetchScalarGridSpec(
            num_scalar_prefetch=1,
            grid=(1,),
            in_specs=[whole((picks // 128, 128)), whole((count, width))],
            out_specs=[whole((cut, width)), whole((groups // 2, cut, width))]
            + [whole((cut, width))] * evens,
            scratch_shapes=[pltpu.VMEM((picks, width), BF16)],
        ),
        out_shape=[piece, jax.ShapeDtypeStruct((groups // 2, cut, width), BF16)] + [piece] * evens,
        compiler_params=params(),
        cost_estimate=cost(2 * picks * count * width, 2 * count * width),
        name="pick_rows",
    )(place, rows.reshape(picks // 128, 128), features)
    return out[0], out[1], out[2:]


def local_kernel(index_ref, values_ref, features_ref, out_ref):
    step = pl.program_id(0)

    @pl.when(step == 0)
    def _():
        out_ref[...] = jnp.zeros_like(out_ref)

    for t in range(TILE_STEP):
        at = step * TILE_STEP + t
        row = pl.ds(pl.multiple_of(index_ref[at, 0] * TILE, TILE), TILE)
        col = pl.ds(pl.multiple_of(index_ref[at, 1] * TILE, TILE), TILE)
        out_ref[row, :] += dot(values_ref[t], features_ref[col, :])


def local_forward(index, values, features):
    tiles = values.shape[0]
    count, width = features.shape
    return pl.pallas_call(
        local_kernel,
        grid_spec=pltpu.PrefetchScalarGridSpec(
            num_scalar_prefetch=1,
            grid=(tiles // TILE_STEP,),
            in_specs=[
                pl.BlockSpec((TILE_STEP, TILE, TILE), lambda i, *_: (i, 0, 0)),
                whole((count, width)),
            ],
            out_specs=whole((count, width)),
        ),
        out_shape=jax.ShapeDtypeStruct((count, width), F32),
        compiler_params=params(),
        cost_estimate=cost(2 * tiles * TILE * TILE * width, 2 * values.size + 6 * features.size),
        name="local_forward",
    )(index, values, features)


def forward_kernel(
    head_count,
    place_ref,
    hub_ref,
    cut_ref,
    local_ref,
    scale_ref,
    features_ref,
    cotangent_ref,
    self_ref,
    neighbor_ref,
    *rest,
):
    hidden_ref, grad_ref, weights_ref, heads, panels, arrived, total = rest[-7:]
    head_refs, own_ref, side_ref = rest[:head_count], rest[head_count], rest[head_count + 1]
    far_refs = rest[head_count + 2 : -7]
    step = pl.program_id(0)
    sections = panels.shape[0] // HUB
    width = features_ref.shape[1]
    cut = own_ref.shape[0]

    @pl.when(step == 0)
    def _():
        total[...] = jnp.zeros_like(total)
        for k, ref in enumerate(head_refs):
            heads[k] = ref[...]
        for s in range(sections):
            panels[s * HUB : (s + 1) * HUB, :] = heads[place_ref[1 + s]]

        def put(k, piece):
            arrived[pl.ds(pl.multiple_of((place_ref[0] ^ k) * cut, cut), cut), :] = piece

        put(0, own_ref[...])
        put(1, side_ref[0])
        for j, ref in enumerate(far_refs):
            put(2 * j + 2, ref[0])
            put(2 * j + 3, ref[1])

    summed = dot(hub_ref[...], panels[...]) + dot(cut_ref[...], arrived[...]) + local_ref[...]
    aggregated = (summed * scale_ref[...]).astype(BF16)
    features = features_ref[...]
    before = dot(features, self_ref[...]) + dot(aggregated, neighbor_ref[...])
    root = 0.7978845608028654
    square = before * before
    bend = jnp.tanh(root * before * (1.0 + 0.044715 * square))
    half = 0.5 + 0.5 * bend
    hidden_ref[...] = (before * half).astype(BF16)
    slope = half + (0.5 * root) * before * (1.0 - bend * bend) * (1.0 + (3 * 0.044715) * square)
    grad = (cotangent_ref[...].astype(F32) * slope).astype(BF16)
    grad_ref[...] = grad
    total[:width, :] += dot(features, grad, ROWS)
    total[width:, :] += dot(aggregated, grad, ROWS)

    @pl.when(step == pl.num_programs(0) - 1)
    def _():
        weights_ref[...] = total[...].astype(BF16)


def forward(place, hub, cut, local, scale, features, cotangent, self_weight, neighbor_weight, heads, pieces):
    count, width = features.shape
    sections = hub.shape[1] // HUB
    flops = 2 * count * width * (hub.shape[1] + cut.shape[1] + 4 * width)
    return pl.pallas_call(
        functools.partial(forward_kernel, len(heads)),
        grid_spec=pltpu.PrefetchScalarGridSpec(
            num_scalar_prefetch=1,
            grid=(count // CHUNK,),
            in_specs=[
                rows_of(CHUNK, hub.shape[1]),
                rows_of(CHUNK, cut.shape[1]),
                rows_of(CHUNK, width),
                rows_of(CHUNK, 1),
                rows_of(CHUNK, width),
                rows_of(CHUNK, width),
                whole((width, width)),
                whole((width, width)),
            ]
            + [whole(x.shape) for x in (*heads, *pieces)],
            out_specs=[rows_of(CHUNK, width), rows_of(CHUNK, width), whole((2 * width, width))],
            scratch_shapes=[
                pltpu.VMEM((len(heads), HUB, width), BF16),
                pltpu.VMEM((sections * HUB, width), BF16),
                pltpu.VMEM((cut.shape[1], width), BF16),
                pltpu.VMEM((2 * width, width), F32),
            ],
        ),
        out_shape=[
            jax.ShapeDtypeStruct((count, width), BF16),
            jax.ShapeDtypeStruct((count, width), BF16),
            jax.ShapeDtypeStruct((2 * width, width), BF16),
        ],
        compiler_params=params(),
        cost_estimate=cost(flops, 2 * hub.size + 2 * cut.size + 14 * features.size),
        name="forward",
    )(place, hub, cut, local, scale, features, cotangent, self_weight, neighbor_weight, *heads, *pieces)


def backward_kernel(
    place_ref,
    hub_ref,
    cut_ref,
    scale_ref,
    grad_ref,
    neighbor_ref,
    aggregate_ref,
    low_ref,
    high_ref,
    own_ref,
    side_ref,
    *rest,
):
    even_refs, far_refs, (hub_total, cut_total, heads) = split_refs(rest, 2 * low_ref.shape[0])
    step = pl.program_id(0)
    sections = hub_ref.shape[1] // HUB
    cut = own_ref.shape[0]

    @pl.when(step == 0)
    def _():
        hub_total[...] = jnp.zeros_like(hub_total)
        cut_total[...] = jnp.zeros_like(cut_total)

    aggregate = (dot(grad_ref[...], neighbor_ref[...], COLS) * scale_ref[...]).astype(BF16)
    aggregate_ref[...] = aggregate
    hub_total[...] += dot(hub_ref[...], aggregate, ROWS)
    cut_total[...] += dot(cut_ref[...], aggregate, ROWS)

    @pl.when(step == pl.num_programs(0) - 1)
    def _():
        heads[...] = jnp.zeros_like(heads)
        for s in range(sections):
            heads[place_ref[1 + s]] += hub_total[s * HUB : (s + 1) * HUB, :]
        half = low_ref.shape[0]
        for j in range(half):
            low_ref[j] = heads[2 * j + 1].astype(BF16)
            high_ref[j] = heads[2 * (half + j) + 1].astype(BF16)
        for j, ref in enumerate(even_refs):
            ref[...] = heads[2 * j].astype(BF16)

        def piece(k):
            at = pl.multiple_of((place_ref[0] ^ k) * cut, cut)
            return cut_total[pl.ds(at, cut), :].astype(BF16)

        own_ref[...] = piece(0)
        for j in range(side_ref.shape[0]):
            side_ref[j] = piece(2 * j + 1)
        for j, ref in enumerate(far_refs):
            ref[...] = piece(2 * j + 2)


def split_refs(refs, first):
    return refs[:first], refs[first:-3], refs[-3:]


def backward(place, hub, cut, scale, grad, neighbor_weight, groups, row_count):
    count, width = grad.shape
    flops = 2 * count * width * (hub.shape[1] + cut.shape[1] + width)
    half = row_count // 4
    width_cut = cut.shape[1] // groups
    outs = [
        (half, HUB, width),
        (half, HUB, width),
        (width_cut, width),
        (groups // 2, width_cut, width),
        *[(HUB, width)] * (row_count // 2),
        *[(width_cut, width)] * (groups // 2 - 1),
    ]
    out = pl.pallas_call(
        backward_kernel,
        grid_spec=pltpu.PrefetchScalarGridSpec(
            num_scalar_prefetch=1,
            grid=(count // CHUNK,),
            in_specs=[
                rows_of(CHUNK, hub.shape[1]),
                rows_of(CHUNK, cut.shape[1]),
                rows_of(CHUNK, 1),
                rows_of(CHUNK, width),
                whole((width, width)),
            ],
            out_specs=[rows_of(CHUNK, width)] + [whole(x) for x in outs],
            scratch_shapes=[
                pltpu.VMEM((hub.shape[1], width), F32),
                pltpu.VMEM((cut.shape[1], width), F32),
                pltpu.VMEM((row_count, HUB, width), F32),
            ],
        ),
        out_shape=[jax.ShapeDtypeStruct(x, BF16) for x in ((count, width), *outs)],
        compiler_params=params(),
        cost_estimate=cost(flops, 2 * hub.size + 2 * cut.size + 4 * grad.size),
        name="backward",
    )(place, hub, cut, scale, grad, neighbor_weight)
    aggregate, low, high, own, side = out[:5]
    return aggregate, low, high, out[5 : 5 + row_count // 2], own, side, out[5 + row_count // 2 :]


def local_back_kernel(index_ref, values_ref, aggregate_ref, grad_ref, self_ref, out_ref):
    step = pl.program_id(0)

    @pl.when(step == 0)
    def _():
        out_ref[...] = dot(grad_ref[...], self_ref[...], COLS)

    for t in range(TILE_STEP):
        at = step * TILE_STEP + t
        row = pl.ds(pl.multiple_of(index_ref[at, 0] * TILE, TILE), TILE)
        col = pl.ds(pl.multiple_of(index_ref[at, 1] * TILE, TILE), TILE)
        out_ref[col, :] += dot(values_ref[t], aggregate_ref[row, :], ROWS)


def local_backward(index, values, aggregate, grad, self_weight):
    tiles = values.shape[0]
    count, width = grad.shape
    return pl.pallas_call(
        local_back_kernel,
        grid_spec=pltpu.PrefetchScalarGridSpec(
            num_scalar_prefetch=1,
            grid=(tiles // TILE_STEP,),
            in_specs=[
                pl.BlockSpec((TILE_STEP, TILE, TILE), lambda i, *_: (i, 0, 0)),
                whole((count, width)),
                whole((count, width)),
                whole((width, width)),
            ],
            out_specs=whole((count, width)),
        ),
        out_shape=jax.ShapeDtypeStruct((count, width), F32),
        compiler_params=params(),
        cost_estimate=cost(
            2 * tiles * TILE * TILE * width + 2 * count * width * width,
            2 * values.size + 8 * grad.size,
        ),
        name="local_backward",
    )(index, values, aggregate, grad, self_weight)


def finish_kernel(piece_count, place_ref, rows_ref, local_ref, low_ref, own_ref, side_ref, *rest):
    out_ref, returned = rest[-2:]
    far_refs, head_refs = rest[:piece_count], rest[piece_count:-2]
    step = pl.program_id(0)
    cut = own_ref.shape[0]
    picks = returned.shape[0]

    @pl.when(step == 0)
    def _():
        def put(k, piece):
            returned[pl.ds(pl.multiple_of((place_ref[0] ^ k) * cut, cut), cut), :] = piece

        put(0, own_ref[...])
        put(1, side_ref[0])
        for j, ref in enumerate(far_refs):
            put(2 * j + 2, ref[0])
            put(2 * j + 3, ref[1])

    where = lax.broadcasted_iota(jnp.int32, (CHUNK, picks), 0) + step * CHUNK
    table = jnp.where(where == rows_ref[...], 1.0, 0.0).astype(BF16)
    total = local_ref[...] + dot(table, returned[...])
    out_ref[...] = total.astype(BF16)

    @pl.when(step == 0)
    def _():
        heads = low_ref[0].astype(F32)
        for ref in head_refs:
            heads = heads + ref[...].astype(F32)
        out_ref[:HUB, :] = (total[:HUB, :] + heads).astype(BF16)


def finish(place, rows, local, low, own, side, far, heads):
    count, width = local.shape
    picks = rows.shape[1]
    return pl.pallas_call(
        functools.partial(finish_kernel, len(far)),
        grid_spec=pltpu.PrefetchScalarGridSpec(
            num_scalar_prefetch=1,
            grid=(count // CHUNK,),
            in_specs=[whole((1, picks)), rows_of(CHUNK, width)]
            + [whole(x.shape) for x in (low, own, side, *far, *heads)],
            out_specs=rows_of(CHUNK, width),
            scratch_shapes=[pltpu.VMEM((picks, width), BF16)],
        ),
        out_shape=jax.ShapeDtypeStruct((count, width), BF16),
        compiler_params=params(),
        cost_estimate=cost(2 * count * picks * width, 6 * local.size),
        name="finish",
    )(place, rows, local, low, own, side, *far, *heads)


def trade(value, axis, k):
    return lax.ppermute(value, axis, [(r, r ^ k) for r in range(lax.axis_size(axis))])


def trade_pieces(side, far):
    side = trade(side, "grp", 1)
    far = [
        trade(jnp.stack([piece, side[j + 1]]), "grp", 2 * j + 2) for j, piece in enumerate(far)
    ]
    return side, far


def on_device(
    features,
    cotangent,
    self_weight,
    neighbor_weight,
    tile_values,
    tile_index,
    hub_adjacency,
    hub_owner,
    send_rows,
    cut_adjacency,
    degrees,
):
    count, width = features.shape
    groups = lax.axis_size("grp")
    row_count = lax.axis_size("row")
    everyone = ("grp", "row")
    device_count = groups * row_count
    values = tile_values[0]
    index = tile_index[0]
    rows = send_rows[0]
    group = lax.axis_index("grp").astype(jnp.int32)
    place = jnp.concatenate([group[None], hub_owner[0] ^ lax.axis_index("row")])

    heads = [features[:HUB]]
    for k in range(2, row_count, 2):
        heads.append(trade(heads[0], "row", k))
    heads = [x for head in heads for x in (head, trade(head, "row", 1))]
    own, side, far = pick_rows(place, rows, features)
    pieces = trade_pieces(side, far)
    scale = lax.rsqrt(degrees.astype(F32))[:, None]
    local = local_forward(index, values, features)
    hidden, grad, weights = forward(
        place, hub_adjacency, cut_adjacency, local, scale, features, cotangent,
        self_weight, neighbor_weight, heads, (own, pieces[0], *pieces[1]),
    )
    parts = lax.all_to_all(weights, everyone, split_axis=0, concat_axis=0, tiled=True)
    aggregate, low, high, evens, own, side, far = backward(
        place, hub_adjacency, cut_adjacency, scale, grad, neighbor_weight, groups, row_count
    )
    half = row_count // 4
    high = trade(high, "row", 1)
    low = trade(low, "row", 1)
    back = [evens[0]]
    for j in reversed(range(1, 2 * half)):
        other = high[j - half] if j >= half else low[j]
        back.append(trade((evens[j].astype(F32) + other.astype(F32)).astype(BF16), "row", 2 * j))
    side, far = trade_pieces(side, far)
    local_grad = local_backward(index, values, aggregate, grad, self_weight)
    summed = jnp.sum(parts.reshape(device_count, -1, width).astype(F32), axis=0).astype(BF16)
    spread = jnp.broadcast_to(summed[None], (device_count, *summed.shape))
    spread = lax.all_to_all(spread, everyone, split_axis=0, concat_axis=0, tiled=True)
    weight_grads = spread.reshape(2 * width, width).astype(F32)
    grad_features = finish(place, rows.reshape(1, -1), local_grad, low, own, side, far, back)
    return hidden, grad_features, weight_grads[:width], weight_grads[width:]


def solution(mesh):
    nodes = P(("grp", "row"), None)
    in_specs = (
        nodes,
        nodes,
        P(),
        P(),
        P(("grp", "row"), None, None, None),
        P(("grp", "row"), None, None),
        nodes,
        P("grp", None),
        P(("grp", "row"), None, None),
        nodes,
        P(("grp", "row")),
    )
    out_specs = (nodes, nodes, P(), P())
    return jax.shard_map(
        on_device, mesh=mesh, in_specs=in_specs, out_specs=out_specs, check_vma=False
    )
```

```python
import jax
import jax.numpy as jnp
from jax import lax
from jax.experimental import pallas as pl
from jax.experimental.pallas import tpu as pltpu
from jax.sharding import PartitionSpec as P

TILE = 128
HUB = 128
CHUNK = 512
VMEM_LIMIT = 40 * 2**20
ROWS = (((0,), (0,)), ((), ()))
COLS = (((1,), (1,)), ((), ()))
F32 = jnp.float32
BF16 = jnp.bfloat16
ANY = pl.BlockSpec(memory_space=pl.ANY)
NEAR = pl.BlockSpec(memory_space=pltpu.VMEM)
SCALARS = pl.BlockSpec(memory_space=pltpu.SMEM)


def call(kernel, name, ins, outs, in_specs, out_specs, scratch, flops, moved):
    return pl.pallas_call(
        kernel,
        in_specs=in_specs,
        out_specs=out_specs,
        out_shape=[jax.ShapeDtypeStruct(shape, dtype) for shape, dtype in outs],
        scratch_shapes=scratch,
        compiler_params=pltpu.CompilerParams(vmem_limit_bytes=VMEM_LIMIT),
        cost_estimate=pl.CostEstimate(flops=flops, bytes_accessed=moved, transcendentals=0),
        name=name,
    )(*ins)


def dot(a, b, dims=(((1,), (0,)), ((), ()))):
    return lax.dot_general(a, b, dims, preferred_element_type=F32)


def aligned(start, size):
    return pl.ds(pl.multiple_of(start, size), size)


def copies(pairs, sems):
    started = [pltpu.make_async_copy(a, b, sems.at[i]) for i, (a, b) in enumerate(pairs)]
    for copy in started:
        copy.start()
    return started


def wait(started):
    for copy in started:
        copy.wait()


def pick_kernel(rows_ref, features_ref, own_ref, *rest):
    out_refs, (picked, sems) = rest[:-2], rest[-2:]
    groups, cut = rows_ref.shape[1:]
    count = features_ref.shape[0]
    group = lax.axis_index("grp")
    across = lax.broadcasted_iota(jnp.int32, (cut, cut), 0)
    along = lax.broadcasted_iota(jnp.int32, (cut, cut), 1)
    columns = []
    for j in range(groups):
        line = jnp.broadcast_to(rows_ref[0, j : j + 1, :].astype(F32), (cut, cut))
        columns.append(jnp.sum(jnp.where(across == along, line, 0.0), axis=1, keepdims=True))
    column = jnp.concatenate(columns, axis=0).astype(jnp.int32)
    where = lax.broadcasted_iota(jnp.int32, (groups * cut, count), 1)
    table = jnp.where(where == column, 1.0, 0.0).astype(BF16)
    picked[...] = dot(table, features_ref[...]).astype(BF16)
    sent = copies(
        [(picked.at[aligned((group ^ (k + 1)) * cut, cut)], ref) for k, ref in enumerate(out_refs)],
        sems,
    )
    own_ref[...] = picked[aligned(group * cut, cut), :]
    wait(sent)


def pick_rows(rows, features):
    _, groups, cut = rows.shape
    count, width = features.shape
    out = call(
        pick_kernel,
        "pick_rows",
        (rows, features),
        [((cut, width), BF16)] * groups,
        [NEAR, NEAR],
        [NEAR] + [ANY] * (groups - 1),
        [pltpu.VMEM((groups * cut, width), BF16), pltpu.SemaphoreType.DMA((groups - 1,))],
        2 * groups * cut * count * width,
        2 * count * width,
    )
    return out


def local_kernel(
    index_ref, values_ref, features_ref, degrees_ref, self_ref, sum_ref, base_ref, scale_ref, turned_ref
):
    count = features_ref.shape[0]
    base_ref[...] = dot(features_ref[...], self_ref[...])
    turned_ref[...] = features_ref[...].T
    scale = lax.rsqrt(degrees_ref[...].astype(F32))
    for j in range(count // TILE):
        line = jnp.broadcast_to(scale[j : j + 1, :], (TILE, TILE))
        scale_ref[j * TILE : (j + 1) * TILE, :] = line.T
    sum_ref[...] = jnp.zeros_like(sum_ref)
    for t in range(values_ref.shape[0]):
        row = aligned(index_ref[0, t, 0] * TILE, TILE)
        col = aligned(index_ref[0, t, 1] * TILE, TILE)
        sum_ref[row, :] += dot(values_ref[t], features_ref[col, :])


def local_forward(index, values, features, degrees, self_weight):
    tiles = values.shape[0]
    count, width = features.shape
    return call(
        local_kernel,
        "local_forward",
        (index, values, features, degrees.reshape(count // TILE, TILE), self_weight),
        [((count, width), F32), ((count, width), F32), ((count, TILE), F32), ((width, count), BF16)],
        [SCALARS, NEAR, NEAR, NEAR, NEAR],
        [NEAR] * 4,
        [],
        2 * tiles * TILE * TILE * width + 2 * count * width * width,
        2 * values.size + 6 * features.size,
    )


def forward_kernel(row_count, groups, *refs):
    owner_ref, hub_ref, cut_ref, local_ref, base_ref, scale_ref, features_ref, turned_ref = refs[:8]
    cotangent_ref, neighbor_ref, own_ref = refs[8:11]
    head_refs = refs[11 : 11 + row_count - 1]
    piece_refs = refs[10 + row_count : 9 + row_count + groups]
    hidden_ref, grad_ref, weights_ref = refs[9 + row_count + groups : 12 + row_count + groups]
    heads, panels, arrived, hidden, aggregated, weights, head_sems, piece_sems, out_sems = refs[
        12 + row_count + groups :
    ]
    sections = panels.shape[0] // HUB
    count, width = features_ref.shape
    cut = own_ref.shape[0]
    group, place = lax.axis_index("grp"), lax.axis_index("row")

    coming = copies([(ref, heads.at[k + 1]) for k, ref in enumerate(head_refs)], head_sems)
    coming += copies(
        [(ref, arrived.at[aligned((group ^ (k + 1)) * cut, cut)]) for k, ref in enumerate(piece_refs)],
        piece_sems,
    )
    heads[0] = features_ref[:HUB, :]
    arrived[aligned(group * cut, cut), :] = own_ref[...]
    wait(coming)
    for s in range(sections):
        panels[s * HUB : (s + 1) * HUB, :] = heads[owner_ref[0, s] ^ place]

    root = 0.7978845608028654
    going = []
    for c in range(count // CHUNK):
        part = slice(c * CHUNK, (c + 1) * CHUNK)
        summed = dot(hub_ref[part, :], panels[...]) + dot(cut_ref[part, :], arrived[...])
        summed = summed + local_ref[part, :]
        scale = jnp.concatenate([scale_ref[part, :]] * (width // TILE), axis=1)
        mixed = (summed * scale).astype(BF16)
        aggregated[part, :] = mixed
        before = base_ref[part, :] + dot(mixed, neighbor_ref[...])
        square = before * before
        bend = jnp.tanh(root * before * (1.0 + 0.044715 * square))
        half = 0.5 + 0.5 * bend
        hidden[part, :] = (before * half).astype(BF16)
        slope = half + (0.5 * root) * before * (1.0 - bend * bend) * (1.0 + (3 * 0.044715) * square)
        grad_ref[part, :] = (cotangent_ref[part, :].astype(F32) * slope).astype(BF16)
        out = pltpu.make_async_copy(hidden.at[part], hidden_ref.at[part], out_sems.at[c])
        out.start()
        going.append(out)
    grad = grad_ref[...]
    weights[:width, :] = dot(turned_ref[...], grad).astype(BF16)
    weights[width:, :] = dot(aggregated[...], grad, ROWS).astype(BF16)
    out = pltpu.make_async_copy(weights, weights_ref, out_sems.at[count // CHUNK])
    out.start()
    wait(going + [out])


def forward(owners, hub, cut, local, base, scale, features, turned, cotangent, neighbor_weight, own, heads, pieces):
    count, width = features.shape
    row_count, groups = len(heads) + 1, len(pieces) + 1
    flops = 2 * count * width * (hub.shape[1] + cut.shape[1] + 3 * width)

    def kernel(*refs):
        forward_kernel(row_count, groups, *refs)

    return call(
        kernel,
        "forward",
        (owners, hub, cut, local, base, scale, features, turned, cotangent, neighbor_weight, own, *heads, *pieces),
        [((count, width), BF16), ((count, width), BF16), ((2 * width, width), BF16)],
        [SCALARS] + [NEAR] * 10 + [ANY] * (row_count + groups - 2),
        [ANY, NEAR, ANY],
        [
            pltpu.VMEM((row_count, HUB, width), BF16),
            pltpu.VMEM((hub.shape[1], width), BF16),
            pltpu.VMEM((cut.shape[1], width), BF16),
            pltpu.VMEM((count, width), BF16),
            pltpu.VMEM((count, width), BF16),
            pltpu.VMEM((2 * width, width), BF16),
            pltpu.SemaphoreType.DMA((row_count - 1,)),
            pltpu.SemaphoreType.DMA((groups - 1,)),
            pltpu.SemaphoreType.DMA((count // CHUNK + 1,)),
        ],
        flops,
        2 * hub.size + 2 * cut.size + 14 * features.size,
    )


def backward_kernel(half, groups, *refs):
    owner_ref, hub_ref, cut_ref, scale_ref, grad_ref, neighbor_ref = refs[:6]
    aggregate_ref, own_ref = refs[6:8]
    even_refs = refs[8 : 8 + half]
    odd_ref = refs[8 + half]
    piece_refs = refs[9 + half : 8 + half + groups]
    heads, odds, back, sems = refs[8 + half + groups :]
    sections = hub_ref.shape[1] // HUB
    width = grad_ref.shape[1]
    cut = own_ref.shape[0]
    group, place = lax.axis_index("grp"), lax.axis_index("row")

    scale = jnp.concatenate([scale_ref[...]] * (width // TILE), axis=1)
    aggregate = (dot(grad_ref[...], neighbor_ref[...], COLS) * scale).astype(BF16)
    aggregate_ref[...] = aggregate
    heads[...] = jnp.zeros_like(heads)
    for s in range(sections):
        heads[owner_ref[0, s] ^ place] += dot(
            hub_ref[:, s * HUB : (s + 1) * HUB], aggregate_ref[...], ROWS
        )
    for j in range(half):
        odds[j] = heads[2 * j + 1].astype(BF16)
    sent = [pltpu.make_async_copy(odds, odd_ref, sems.at[0])]
    sent[0].start()
    for j, ref in enumerate(even_refs):
        ref[...] = heads[2 * j].astype(BF16)
    back[...] = dot(cut_ref[...], aggregate_ref[...], ROWS).astype(BF16)
    for k, ref in enumerate(piece_refs):
        piece = back.at[aligned((group ^ (k + 1)) * cut, cut)]
        sent.append(pltpu.make_async_copy(piece, ref, sems.at[k + 1]))
        sent[-1].start()
    own_ref[...] = back[aligned(group * cut, cut), :]
    wait(sent)


def backward(owners, hub, cut, scale, grad, neighbor_weight, groups, row_count):
    count, width = grad.shape
    half = row_count // 2
    piece = cut.shape[1] // groups

    def kernel(*refs):
        backward_kernel(half, groups, *refs)

    out = call(
        kernel,
        "backward",
        (owners, hub, cut, scale, grad, neighbor_weight),
        [((count, width), BF16), ((piece, width), BF16)]
        + [((HUB, width), BF16)] * half
        + [((half, HUB, width), BF16)]
        + [((piece, width), BF16)] * (groups - 1),
        [SCALARS] + [NEAR] * 5,
        [NEAR] * (2 + half) + [ANY] * groups,
        [
            pltpu.VMEM((row_count, HUB, width), F32),
            pltpu.VMEM((half, HUB, width), BF16),
            pltpu.VMEM((cut.shape[1], width), BF16),
            pltpu.SemaphoreType.DMA((groups,)),
        ],
        2 * count * width * (hub.shape[1] + cut.shape[1] + width),
        2 * hub.size + 2 * cut.size + 4 * grad.size,
    )
    return out[0], out[1], out[2 : 2 + half], out[2 + half], out[3 + half :]


def local_back_kernel(index_ref, values_ref, aggregate_ref, grad_ref, self_ref, out_ref):
    out_ref[...] = dot(grad_ref[...], self_ref[...], COLS)
    for t in range(values_ref.shape[0]):
        row = aligned(index_ref[0, t, 0] * TILE, TILE)
        col = aligned(index_ref[0, t, 1] * TILE, TILE)
        out_ref[col, :] += dot(values_ref[t], aggregate_ref[row, :], ROWS)


def local_backward(index, values, aggregate, grad, self_weight):
    tiles = values.shape[0]
    count, width = grad.shape
    return call(
        local_back_kernel,
        "local_backward",
        (index, values, aggregate, grad, self_weight),
        [((count, width), F32)],
        [SCALARS] + [NEAR] * 4,
        [NEAR],
        [],
        2 * tiles * TILE * TILE * width + 2 * count * width * width,
        2 * values.size + 8 * grad.size,
    )[0]


def finish_kernel(groups, *refs):
    rows_ref, local_ref, own_ref, mine_ref, side_ref = refs[:5]
    piece_refs = refs[5 : 4 + groups]
    head_refs = refs[4 + groups : -7]
    out_ref, returned, side, heads, result, sems, out_sems = refs[-7:]
    cut = own_ref.shape[0]
    count = local_ref.shape[0]
    picks = returned.shape[0]
    group = lax.axis_index("grp")

    coming = copies(
        [
            (ref, returned.at[aligned((group ^ (k + 1)) * cut, cut)])
            for k, ref in enumerate(piece_refs)
        ]
        + [(side_ref.at[0], side)]
        + [(ref, heads.at[k]) for k, ref in enumerate(head_refs)],
        sems,
    )
    returned[aligned(group * cut, cut), :] = own_ref[...]
    rows = jnp.concatenate([rows_ref[0, j : j + 1, :] for j in range(groups)], axis=1)
    wait(coming)
    going = []
    for c in range(count // CHUNK):
        part = slice(c * CHUNK, (c + 1) * CHUNK)
        where = lax.broadcasted_iota(jnp.int32, (CHUNK, picks), 0) + c * CHUNK
        table = jnp.where(where == rows, 1.0, 0.0).astype(BF16)
        total = local_ref[part, :] + dot(table, returned[...])
        result[part, :] = total.astype(BF16)
        if c == 0:
            extra = mine_ref[...].astype(F32) + side[...].astype(F32)
            for k in range(len(head_refs)):
                extra = extra + heads[k].astype(F32)
            result[:HUB, :] = (total[:HUB, :] + extra).astype(BF16)
        out = pltpu.make_async_copy(result.at[part], out_ref.at[part], out_sems.at[c])
        out.start()
        going.append(out)
    wait(going)


def finish(rows, local, own, mine, side, pieces, heads):
    count, width = local.shape
    groups = rows.shape[1]
    picks = groups * rows.shape[2]

    def kernel(*refs):
        finish_kernel(groups, *refs)

    return call(
        kernel,
        "finish",
        (rows, local, own, mine, side, *pieces, *heads),
        [((count, width), BF16)],
        [NEAR] * 4 + [ANY] * (1 + len(pieces) + len(heads)),
        [ANY],
        [
            pltpu.VMEM((picks, width), BF16),
            pltpu.VMEM((HUB, width), BF16),
            pltpu.VMEM((len(heads), HUB, width), BF16),
            pltpu.VMEM((count, width), BF16),
            pltpu.SemaphoreType.DMA((1 + len(pieces) + len(heads),)),
            pltpu.SemaphoreType.DMA((count // CHUNK,)),
        ],
        2 * count * picks * width,
        6 * local.size,
    )[0]


def trade(value, axis, k):
    return lax.ppermute(value, axis, [(r, r ^ k) for r in range(lax.axis_size(axis))])


def on_device(
    features,
    cotangent,
    self_weight,
    neighbor_weight,
    tile_values,
    tile_index,
    hub_adjacency,
    hub_owner,
    send_rows,
    cut_adjacency,
    degrees,
):
    count, width = features.shape
    groups = lax.axis_size("grp")
    row_count = lax.axis_size("row")
    everyone = ("grp", "row")
    device_count = groups * row_count
    values = tile_values[0]

    head = features[:HUB]
    evens = [head] + [trade(head, "row", k) for k in range(2, row_count, 2)]
    heads = [x for even in evens for x in (even, trade(even, "row", 1))][1:]
    own, *pieces = pick_rows(send_rows, features)
    pieces = [trade(piece, "grp", k + 1) for k, piece in enumerate(pieces)]
    local, base, scale, turned = local_forward(tile_index, values, features, degrees, self_weight)
    hidden, grad, weights = forward(
        hub_owner, hub_adjacency, cut_adjacency, local, base, scale, features, turned,
        cotangent, neighbor_weight, own, heads, pieces,
    )
    parts = lax.all_to_all(weights, everyone, split_axis=0, concat_axis=0, tiled=True)
    aggregate, own, evens, odds, pieces = backward(
        hub_owner, hub_adjacency, cut_adjacency, scale, grad, neighbor_weight, groups, row_count
    )
    odds = trade(odds, "row", 1)
    heads = [
        trade((even.astype(F32) + odds[j + 1].astype(F32)).astype(BF16), "row", 2 * j + 2)
        for j, even in enumerate(evens[1:])
    ]
    pieces = [trade(piece, "grp", k + 1) for k, piece in enumerate(pieces)]
    local_grad = local_backward(tile_index, values, aggregate, grad, self_weight)
    summed = jnp.sum(parts.reshape(device_count, -1, width).astype(F32), axis=0).astype(BF16)
    spread = jnp.broadcast_to(summed[None], (device_count, *summed.shape))
    spread = lax.all_to_all(spread, everyone, split_axis=0, concat_axis=0, tiled=True)
    weight_grads = spread.reshape(2 * width, width).astype(F32)
    grad_features = finish(send_rows, local_grad, own, evens[0], odds, pieces, heads)
    return hidden, grad_features, weight_grads[:width], weight_grads[width:]


def solution(mesh):
    nodes = P(("grp", "row"), None)
    in_specs = (
        nodes,
        nodes,
        P(),
        P(),
        P(("grp", "row"), None, None, None),
        P(("grp", "row"), None, None),
        nodes,
        P("grp", None),
        P(("grp", "row"), None, None),
        nodes,
        P(("grp", "row")),
    )
    out_specs = (nodes, nodes, P(), P())
    return jax.shard_map(
        on_device, mesh=mesh, in_specs=in_specs, out_specs=out_specs, check_vma=False
    )
```

```python
import jax
import jax.numpy as jnp
from jax import lax
from jax.experimental import pallas as pl
from jax.experimental.pallas import tpu as pltpu
from jax.sharding import PartitionSpec as P

TILE = 128
HUB = 128
CHUNK = 512
TILE_STEP = 16
VMEM_LIMIT = 62 * 2**20
ROWS = (((0,), (0,)), ((), ()))
COLS = (((1,), (1,)), ((), ()))
F32 = jnp.float32
BF16 = jnp.bfloat16
ANY = pl.BlockSpec(memory_space=pl.ANY)
NEAR = pl.BlockSpec(memory_space=pltpu.VMEM)
SCALARS = pl.BlockSpec(memory_space=pltpu.SMEM)


def call(kernel, name, ins, outs, in_specs, out_specs, scratch, flops, moved):
    return pl.pallas_call(
        kernel,
        in_specs=in_specs,
        out_specs=out_specs,
        out_shape=[jax.ShapeDtypeStruct(shape, dtype) for shape, dtype in outs],
        scratch_shapes=scratch,
        compiler_params=pltpu.CompilerParams(vmem_limit_bytes=VMEM_LIMIT),
        cost_estimate=pl.CostEstimate(flops=flops, bytes_accessed=moved, transcendentals=0),
        name=name,
    )(*ins)


def dot(a, b, dims=(((1,), (0,)), ((), ()))):
    return lax.dot_general(a, b, dims, preferred_element_type=F32)


def aligned(start, size):
    return pl.ds(pl.multiple_of(start, size), size)


class Mover:
    def __init__(self, sems):
        self.sems, self.used, self.out = sems, 0, []

    def get(self, source, target):
        copy = pltpu.make_async_copy(source, target, self.sems.at[self.used])
        self.used += 1
        copy.start()
        return copy

    def put(self, source, target):
        self.out.append(self.get(source, target))

    def drain(self):
        wait(self.out)


def wait(started):
    for copy in started:
        copy.wait()


def split(count, step):
    return [slice(i, i + step) for i in range(0, count, step)]


def pick_kernel(rows_ref, features_ref, head_ref, *rest):
    out_refs, (features, picked, sems) = rest[:-3], rest[-3:]
    groups, cut = rows_ref.shape[1:]
    count = features_ref.shape[0]
    group = lax.axis_index("grp")
    mover = Mover(sems)
    parts = split(count, CHUNK)
    coming = [mover.get(features_ref.at[part], features.at[part]) for part in parts]
    across = lax.broadcasted_iota(jnp.int32, (cut, cut), 0)
    along = lax.broadcasted_iota(jnp.int32, (cut, cut), 1)
    columns = []
    for j in range(groups):
        line = jnp.broadcast_to(rows_ref[0, j : j + 1, :].astype(F32), (cut, cut))
        columns.append(jnp.sum(jnp.where(across == along, line, 0.0), axis=1, keepdims=True))
    column = jnp.concatenate(columns, axis=0).astype(jnp.int32)
    where = lax.broadcasted_iota(jnp.int32, (groups * cut, count), 1)
    table = jnp.where(where == column, 1.0, 0.0).astype(BF16)
    wait(coming)
    mover.put(features.at[:HUB], head_ref)
    picked[...] = dot(table, features[...]).astype(BF16)
    for k, ref in enumerate(out_refs):
        mover.put(picked.at[aligned((group ^ k) * cut, cut)], ref)
    mover.drain()


def pick_rows(rows, features):
    _, groups, cut = rows.shape
    count, width = features.shape
    return call(
        pick_kernel,
        "pick_rows",
        (rows, features),
        [((HUB, width), BF16)] + [((cut, width), BF16)] * groups,
        [NEAR, ANY],
        [ANY] * (1 + groups),
        [
            pltpu.VMEM((count, width), BF16),
            pltpu.VMEM((groups * cut, width), BF16),
            pltpu.SemaphoreType.DMA((1 + groups + count // CHUNK,)),
        ],
        2 * groups * cut * count * width,
        2 * count * width,
    )


def scale_of(degrees_ref, part, width):
    lines = lax.rsqrt(degrees_ref[part.start // TILE : part.stop // TILE, :].astype(F32))
    blocks = [
        jnp.broadcast_to(lines[j : j + 1, :], (TILE, TILE)).T for j in range(lines.shape[0])
    ]
    return jnp.concatenate([jnp.concatenate(blocks, axis=0)] * (width // TILE), axis=1)


def block_kernel(row_count, groups, *refs):
    index_ref, owner_ref, degrees_ref, self_ref, neighbor_ref = refs[:5]
    features_ref, values_ref, hub_ref, cut_ref, cotangent_ref = refs[5:10]
    head_refs = refs[10 : 9 + row_count]
    piece_refs = refs[9 + row_count : 9 + row_count + groups]
    outs = refs[9 + row_count + groups : -17]
    hidden_ref, grad_ref, aggregate_ref, weights_ref, odd_ref = outs[:5]
    even_refs, back_refs = outs[5 : 5 + row_count // 2], outs[5 + row_count // 2 :]
    features, values, hub, cut, cotangent, heads, panels, arrived = refs[-17:-9]
    total, hidden, grad, aggregated, aggregate, weights, sums, back, sems = refs[-9:]
    sections = panels.shape[0] // HUB
    count, width = features_ref.shape
    size = piece_refs[0].shape[0]
    group, place = lax.axis_index("grp"), lax.axis_index("row")

    mover = Mover(sems)
    parts = split(count, CHUNK)
    steps = split(values_ref.shape[0], TILE_STEP)
    rows = [mover.get(features_ref.at[part], features.at[part]) for part in parts]
    tiles = [mover.get(values_ref.at[part], values.at[part]) for part in steps]
    first = [mover.get(ref, heads.at[k + 1]) for k, ref in enumerate(head_refs)]
    first += [
        mover.get(ref, arrived.at[aligned((group ^ k) * size, size)])
        for k, ref in enumerate(piece_refs)
    ]
    coming = []
    for part in parts:
        pairs = [(hub_ref, hub), (cut_ref, cut), (cotangent_ref, cotangent)]
        coming.append([mover.get(a.at[part], b.at[part]) for a, b in pairs])

    total[...] = jnp.zeros_like(total)
    wait(rows)
    for part, copy in zip(steps, tiles):
        copy.wait()
        for t in range(part.start, part.stop):
            row = aligned(index_ref[0, 0, t] * TILE, TILE)
            col = aligned(index_ref[0, 1, t] * TILE, TILE)
            total[row, :] += dot(values[t], features[col, :])

    wait(first)
    heads[0] = features[:HUB, :]
    for s in range(sections):
        panels[s * HUB : (s + 1) * HUB, :] = heads[owner_ref[0, s] ^ place]
    root = 0.7978845608028654
    for part, copies in zip(parts, coming):
        scale = scale_of(degrees_ref, part, width)
        wait(copies)
        summed = dot(hub[part, :], panels[...]) + dot(cut[part, :], arrived[...])
        mixed = ((summed + total[part, :]) * scale).astype(BF16)
        aggregated[part, :] = mixed
        before = dot(features[part, :], self_ref[...]) + dot(mixed, neighbor_ref[...])
        square = before * before
        bend = jnp.tanh(root * before * (1.0 + 0.044715 * square))
        half = 0.5 + 0.5 * bend
        hidden[part, :] = (before * half).astype(BF16)
        slope = half + (0.5 * root) * before * (1.0 - bend * bend) * (1.0 + (3 * 0.044715) * square)
        new = (cotangent[part, :].astype(F32) * slope).astype(BF16)
        grad[part, :] = new
        aggregate[part, :] = (dot(new, neighbor_ref[...], COLS) * scale).astype(BF16)
        mover.put(hidden.at[part], hidden_ref.at[part])
        mover.put(grad.at[part], grad_ref.at[part])
        mover.put(aggregate.at[part], aggregate_ref.at[part])
    weights[:width, :] = dot(features[...], grad[...], ROWS).astype(BF16)
    weights[width:, :] = dot(aggregated[...], grad[...], ROWS).astype(BF16)
    mover.put(weights, weights_ref)
    sums[...] = jnp.zeros_like(sums)
    returns = dot(hub[...], aggregate[...], ROWS)
    for s in range(sections):
        sums[owner_ref[0, s] ^ place] += returns[s * HUB : (s + 1) * HUB, :]
    for j in list(range(1, row_count, 2)) + list(range(0, row_count, 2)):
        heads[j] = sums[j].astype(BF16)
        mover.put(heads.at[j], odd_ref.at[j // 2] if j % 2 else even_refs[j // 2])
    back[...] = dot(cut[...], aggregate[...], ROWS).astype(BF16)
    for k, ref in enumerate(back_refs):
        mover.put(back.at[aligned((group ^ k) * size, size)], ref)
    mover.drain()


def block(index, owners, degrees, self_weight, neighbor_weight, features, values, hub, cut, cotangent, heads, pieces):
    count, width = features.shape
    tiles = values.shape[0]
    row_count, groups = len(heads) + 1, len(pieces)
    half = row_count // 2
    piece = cut.shape[1] // groups
    flops = 2 * count * width * (2 * hub.shape[1] + 2 * cut.shape[1] + 5 * width)
    near = pltpu.VMEM((count, width), BF16)

    def kernel(*refs):
        block_kernel(row_count, groups, *refs)

    out = call(
        kernel,
        "block",
        (
            index, owners, degrees, self_weight, neighbor_weight,
            features, values, hub, cut, cotangent, *heads, *pieces,
        ),
        [((count, width), BF16)] * 3
        + [((2 * width, width), BF16), ((half, HUB, width), BF16)]
        + [((HUB, width), BF16)] * half
        + [((piece, width), BF16)] * groups,
        [SCALARS, SCALARS, NEAR, NEAR, NEAR] + [ANY] * (5 + len(heads) + groups),
        [ANY] * (5 + half + groups),
        [
            near,
            pltpu.VMEM(values.shape, BF16),
            pltpu.VMEM(hub.shape, BF16),
            pltpu.VMEM(cut.shape, BF16),
            near,
            pltpu.VMEM((row_count, HUB, width), BF16),
            pltpu.VMEM((hub.shape[1], width), BF16),
            pltpu.VMEM((cut.shape[1], width), BF16),
            pltpu.VMEM((count, width), F32),
            near,
            near,
            near,
            near,
            pltpu.VMEM((2 * width, width), BF16),
            pltpu.VMEM((row_count, HUB, width), F32),
            pltpu.VMEM((cut.shape[1], width), BF16),
            pltpu.SemaphoreType.DMA(
                (7 * count // CHUNK + tiles // TILE_STEP + 2 * row_count + 2 * groups,)
            ),
        ],
        flops + 2 * tiles * TILE * TILE * width,
        2 * hub.size + 2 * cut.size + 2 * values.size + 14 * features.size,
    )
    hidden, grad, aggregate, weights, odds = out[:5]
    return hidden, grad, aggregate, weights, odds, out[5 : 5 + half], out[5 + half :]


def local_back_kernel(groups, *refs):
    index_ref, self_ref, rows_ref, values_ref, aggregate_ref, grad_ref = refs[:6]
    piece_refs = refs[6 : 6 + groups]
    out_ref, head_ref, values, aggregate, grad, returned, total, result, sems = refs[6 + groups :]
    size = piece_refs[0].shape[0]
    picks = returned.shape[0]
    group = lax.axis_index("grp")

    mover = Mover(sems)
    parts = split(grad_ref.shape[0], CHUNK)
    first = [mover.get(grad_ref.at[part], grad.at[part]) for part in parts]
    back = [
        mover.get(ref, returned.at[aligned((group ^ k) * size, size)])
        for k, ref in enumerate(piece_refs)
    ]
    coming = [mover.get(aggregate_ref.at[part], aggregate.at[part]) for part in parts]
    steps = split(values_ref.shape[0], TILE_STEP)
    tiles = [mover.get(values_ref.at[part], values.at[part]) for part in steps]
    rows = jnp.concatenate([rows_ref[0, j : j + 1, :] for j in range(groups)], axis=1)
    wait(back)
    for part, copy in zip(parts, first):
        where = lax.broadcasted_iota(jnp.int32, (CHUNK, picks), 0) + part.start
        table = jnp.where(where == rows, 1.0, 0.0).astype(BF16)
        copy.wait()
        total[part, :] = dot(grad[part, :], self_ref[...], COLS) + dot(table, returned[...])
    wait(coming)
    for part, copy in zip(steps, tiles):
        copy.wait()
        for t in range(part.start, part.stop):
            row = aligned(index_ref[0, 0, t] * TILE, TILE)
            col = aligned(index_ref[0, 1, t] * TILE, TILE)
            total[col, :] += dot(values[t], aggregate[row, :], ROWS)
    mover.put(total.at[:HUB], head_ref)
    for part in parts:
        result[part, :] = total[part, :].astype(BF16)
        mover.put(result.at[part], out_ref.at[part])
    mover.drain()


def local_backward(index, self_weight, rows, values, aggregate, grad, pieces):
    tiles = values.shape[0]
    count, width = grad.shape
    groups = len(pieces)
    picks = groups * rows.shape[2]
    near = pltpu.VMEM((count, width), BF16)

    def kernel(*refs):
        local_back_kernel(groups, *refs)

    return call(
        kernel,
        "local_backward",
        (index, self_weight, rows, values, aggregate, grad, *pieces),
        [((count, width), BF16), ((HUB, width), F32)],
        [SCALARS, NEAR, NEAR] + [ANY] * (3 + groups),
        [ANY, ANY],
        [
            pltpu.VMEM(values.shape, BF16),
            near,
            near,
            pltpu.VMEM((picks, width), BF16),
            pltpu.VMEM((count, width), F32),
            near,
            pltpu.SemaphoreType.DMA((3 * count // CHUNK + groups + tiles // TILE_STEP + 1,)),
        ],
        2 * tiles * TILE * TILE * width + 2 * count * width * (width + picks),
        2 * values.size + 8 * grad.size,
    )


def finish_kernel(grad_ref, local_ref, weights_ref, mine_ref, side_ref, *refs):
    head_refs = refs[:-8]
    out_ref, self_ref, neighbor_ref, local, weights, sums, heads, sems = refs[-8:]
    width = weights_ref.shape[1]
    mover = Mover(sems)
    ends = [mine_ref, side_ref.at[0], *head_refs]
    first = [mover.get(local_ref, local)]
    first += [mover.get(ref, heads.at[k]) for k, ref in enumerate(ends)]
    mover.get(weights_ref, weights).wait()
    sums[...] = weights[...].astype(F32)
    mover.put(sums.at[:width], self_ref)
    mover.put(sums.at[width:], neighbor_ref)
    wait(first)
    total = local[...] + jnp.sum(heads[...].astype(F32), axis=0)
    heads[0] = total.astype(BF16)
    mover.put(heads.at[0], out_ref.at[:HUB])
    mover.drain()


def finish(grad, local, weights, mine, side, heads):
    width = grad.shape[1]
    return pl.pallas_call(
        finish_kernel,
        in_specs=[ANY] * (5 + len(heads)),
        out_specs=[ANY] * 3,
        out_shape=[
            jax.ShapeDtypeStruct(grad.shape, BF16),
            jax.ShapeDtypeStruct((width, width), F32),
            jax.ShapeDtypeStruct((width, width), F32),
        ],
        scratch_shapes=[
            pltpu.VMEM((HUB, width), F32),
            pltpu.VMEM((2 * width, width), BF16),
            pltpu.VMEM((2 * width, width), F32),
            pltpu.VMEM((len(heads) + 2, HUB, width), BF16),
            pltpu.SemaphoreType.DMA((len(heads) + 7,)),
        ],
        input_output_aliases={0: 0},
        compiler_params=pltpu.CompilerParams(vmem_limit_bytes=VMEM_LIMIT),
        cost_estimate=pl.CostEstimate(flops=weights.size, bytes_accessed=8 * weights.size, transcendentals=0),
        name="finish",
    )(grad, local, weights, mine, side, *heads)


def trade(value, axis, k):
    return lax.ppermute(value, axis, [(r, r ^ k) for r in range(lax.axis_size(axis))])


def on_device(
    features,
    cotangent,
    self_weight,
    neighbor_weight,
    tile_values,
    tile_index,
    hub_adjacency,
    hub_owner,
    send_rows,
    cut_adjacency,
    degrees,
):
    count, width = features.shape
    groups = lax.axis_size("grp")
    row_count = lax.axis_size("row")
    everyone = ("grp", "row")
    values = tile_values[0]
    index = tile_index.transpose(0, 2, 1)
    degrees = degrees.reshape(count // TILE, TILE)

    head, *pieces = pick_rows(send_rows, features)
    evens = [head] + [trade(head, "row", k) for k in range(2, row_count, 2)]
    heads = [x for even in evens for x in (even, trade(even, "row", 1))][1:]
    pieces = [pieces[0]] + [trade(pieces[k], "grp", k) for k in range(1, groups)]
    hidden, grad, aggregate, weights, odds, evens, pieces = block(
        index, hub_owner, degrees, self_weight, neighbor_weight, features, values,
        hub_adjacency, cut_adjacency, cotangent, heads, pieces,
    )
    parts = weights.reshape(groups * row_count, -1, width)
    parts = lax.all_to_all(parts, everyone, split_axis=0, concat_axis=0, tiled=True)
    odds = trade(odds, "row", 1)
    heads = [
        trade((even.astype(F32) + odds[j + 1].astype(F32)).astype(BF16), "row", 2 * j + 2)
        for j, even in enumerate(evens[1:])
    ]
    pieces = [pieces[0]] + [trade(pieces[k], "grp", k) for k in range(1, groups)]
    parts, pieces = lax.optimization_barrier((parts, pieces))
    sums = jnp.sum(parts.astype(F32), axis=0).astype(BF16)
    sums = jnp.broadcast_to(sums[None], parts.shape)
    sums = lax.all_to_all(sums, everyone, split_axis=0, concat_axis=0, tiled=True)
    grad_features, head = local_backward(
        index, self_weight, send_rows, values, aggregate, grad, pieces
    )
    grad_features, grad_self, grad_neighbor = finish(
        grad_features, head, sums.reshape(2 * width, width), evens[0], odds, heads
    )
    return hidden, grad_features, grad_self, grad_neighbor


def solution(mesh):
    nodes = P(("grp", "row"), None)
    in_specs = (
        nodes,
        nodes,
        P(),
        P(),
        P(("grp", "row"), None, None, None),
        P(("grp", "row"), None, None),
        nodes,
        P("grp", None),
        P(("grp", "row"), None, None),
        nodes,
        P(("grp", "row")),
    )
    out_specs = (nodes, nodes, P(), P())
    return jax.shard_map(
        on_device, mesh=mesh, in_specs=in_specs, out_specs=out_specs, check_vma=False
    )
```

```python
import jax
import jax.numpy as jnp
from jax import lax
from jax.experimental import pallas as pl
from jax.experimental.pallas import tpu as pltpu
from jax.sharding import PartitionSpec as P

TILE = 128
HUB = 128
CHUNK = 1024
TILE_STEP = 32
VMEM_LIMIT = 62 * 2**20
ROWS = (((0,), (0,)), ((), ()))
COLS = (((1,), (1,)), ((), ()))
F32 = jnp.float32
BF16 = jnp.bfloat16
ANY = pl.BlockSpec(memory_space=pl.ANY)
NEAR = pl.BlockSpec(memory_space=pltpu.VMEM)
SCALARS = pl.BlockSpec(memory_space=pltpu.SMEM)


def call(kernel, name, ins, outs, in_specs, out_specs, scratch, flops, moved):
    return pl.pallas_call(
        kernel,
        in_specs=in_specs,
        out_specs=out_specs,
        out_shape=[jax.ShapeDtypeStruct(shape, dtype) for shape, dtype in outs],
        scratch_shapes=scratch,
        compiler_params=pltpu.CompilerParams(vmem_limit_bytes=VMEM_LIMIT),
        cost_estimate=pl.CostEstimate(flops=flops, bytes_accessed=moved, transcendentals=0),
        name=name,
    )(*ins)


def dot(a, b, dims=(((1,), (0,)), ((), ()))):
    return lax.dot_general(a, b, dims, preferred_element_type=F32)


def aligned(start, size):
    return pl.ds(pl.multiple_of(start, size), size)


class Mover:
    def __init__(self, sems):
        self.sems, self.used, self.out = sems, 0, []

    def get(self, source, target):
        copy = pltpu.make_async_copy(source, target, self.sems.at[self.used])
        self.used += 1
        copy.start()
        return copy

    def put(self, source, target):
        self.out.append(self.get(source, target))

    def drain(self):
        wait(self.out)


def wait(started):
    for copy in started:
        copy.wait()


def split(count, step):
    return [slice(i, i + step) for i in range(0, count, step)]


def pick_kernel(rows_ref, features_ref, head_ref, *rest):
    out_refs, (features, picked, sems) = rest[:-3], rest[-3:]
    groups, cut = rows_ref.shape[1:]
    count = features_ref.shape[0]
    group = lax.axis_index("grp")
    mover = Mover(sems)
    parts = split(count, CHUNK)
    coming = [mover.get(features_ref.at[part], features.at[part]) for part in parts]
    across = lax.broadcasted_iota(jnp.int32, (cut, cut), 0)
    along = lax.broadcasted_iota(jnp.int32, (cut, cut), 1)
    columns = []
    for j in range(groups):
        line = jnp.broadcast_to(rows_ref[0, j : j + 1, :].astype(F32), (cut, cut))
        columns.append(jnp.sum(jnp.where(across == along, line, 0.0), axis=1, keepdims=True))
    column = jnp.concatenate(columns, axis=0).astype(jnp.int32)
    where = lax.broadcasted_iota(jnp.int32, (groups * cut, count), 1)
    table = jnp.where(where == column, 1.0, 0.0).astype(BF16)
    wait(coming)
    mover.put(features.at[:HUB], head_ref)
    picked[...] = dot(table, features[...]).astype(BF16)
    odd_ref, even_refs = out_refs[0], out_refs[1:]
    for k in range(groups):
        ref = odd_ref.at[k // 2] if k % 2 else even_refs[k // 2]
        mover.put(picked.at[aligned((group ^ k) * cut, cut)], ref)
    mover.drain()


def pick_rows(rows, features):
    _, groups, cut = rows.shape
    count, width = features.shape
    return call(
        pick_kernel,
        "pick_rows",
        (rows, features),
        [((HUB, width), BF16), ((groups // 2, cut, width), BF16)]
        + [((cut, width), BF16)] * (groups // 2),
        [NEAR, ANY],
        [ANY] * (2 + groups // 2),
        [
            pltpu.VMEM((count, width), BF16),
            pltpu.VMEM((groups * cut, width), BF16),
            pltpu.SemaphoreType.DMA((1 + groups + count // CHUNK,)),
        ],
        2 * groups * cut * count * width,
        2 * count * width,
    )


def scale_of(degrees_ref, part, width):
    lines = lax.rsqrt(degrees_ref[part.start // TILE : part.stop // TILE, :].astype(F32))
    blocks = [
        jnp.broadcast_to(lines[j : j + 1, :], (TILE, TILE)).T for j in range(lines.shape[0])
    ]
    return jnp.concatenate([jnp.concatenate(blocks, axis=0)] * (width // TILE), axis=1)


def block_kernel(row_count, groups, *refs):
    index_ref, owner_ref, degrees_ref, self_ref, neighbor_ref = refs[:5]
    features_ref, values_ref, hub_ref, cut_ref, cotangent_ref = refs[5:10]
    head_refs = refs[10 : 9 + row_count]
    piece_refs = refs[9 + row_count : 9 + row_count + groups]
    outs = refs[9 + row_count + groups : -15]
    hidden_ref, grad_ref, aggregate_ref, weights_ref, odd_ref = outs[:5]
    even_refs, back_refs = outs[5 : 5 + row_count // 2], outs[5 + row_count // 2 :]
    pair, stack, values, edges, cotangent, heads, panels = refs[-15:-8]
    total, hidden, grad, aggregate, weights, sums, back, sems = refs[-8:]
    count, width = features_ref.shape
    depth = hub_ref.shape[1]
    sections = depth // HUB
    size = piece_refs[0].shape[0]
    group, place = lax.axis_index("grp"), lax.axis_index("row")

    mover = Mover(sems)
    parts = split(count, CHUNK)
    steps = split(values_ref.shape[0], TILE_STEP)
    rows = [mover.get(features_ref, pair.at[:, :width])]
    tiles = [mover.get(values_ref.at[part], values.at[part]) for part in steps]
    first = [mover.get(ref, heads.at[k + 1]) for k, ref in enumerate(head_refs)]
    for k in range(groups):
        ref = piece_refs[groups // 2 + k // 2].at[k // 2] if k % 2 else piece_refs[k // 2]
        first.append(mover.get(ref, panels.at[aligned(depth + (group ^ k) * size, size)]))
    first += [
        mover.get(self_ref, stack.at[:width]), mover.get(neighbor_ref, stack.at[width:])
    ]
    coming = []
    for part in parts:
        coming.append([
            mover.get(hub_ref.at[part], edges.at[part, :depth]),
            mover.get(cut_ref.at[part], edges.at[part, depth:]),
            mover.get(cotangent_ref.at[part], cotangent.at[part]),
        ])

    total[...] = jnp.zeros_like(total)
    wait(rows)
    for part, copy in zip(steps, tiles):
        copy.wait()
        for t in range(part.start, part.stop):
            row = aligned(index_ref[0, 0, t] * TILE, TILE)
            col = aligned(index_ref[0, 1, t] * TILE, TILE)
            total[row, :] += dot(values[t], pair[col, :width])

    wait(first)
    heads[0] = pair[:HUB, :width]
    for s in range(sections):
        panels[s * HUB : (s + 1) * HUB, :] = heads[owner_ref[0, s] ^ place]
    neighbor = stack[width:, :]
    root, bend = 0.7978845608028654, 0.044715
    for part, copies in zip(parts, coming):
        wait(copies)
        scale = scale_of(degrees_ref, part, width)
        summed = total[part, :] + dot(edges[part, :], panels[...])
        pair[part, width:] = (summed * scale).astype(BF16)
        before = dot(pair[part, :], stack[...])
        slope = (root * bend) * (before * before) + root
        wave = jnp.tanh(before * slope)
        half = 0.5 * wave + 0.5
        hidden[part, :] = (before * half).astype(BF16)
        rise = half + (before * (1.5 * slope - root)) * (1.0 - wave * wave)
        new = (cotangent[part, :].astype(F32) * rise).astype(BF16)
        grad[part, :] = new
        aggregate[part, :] = (dot(new, neighbor, COLS) * scale).astype(BF16)
        mover.put(hidden.at[part], hidden_ref.at[part])
        mover.put(grad.at[part], grad_ref.at[part])
        mover.put(aggregate.at[part], aggregate_ref.at[part])
    weights[...] = dot(pair[...], grad[...], ROWS).astype(BF16)
    mover.put(weights, weights_ref)
    sums[...] = jnp.zeros_like(sums)
    returns = dot(edges[...], aggregate[...], ROWS)
    for s in range(sections):
        sums[owner_ref[0, s] ^ place] += returns[s * HUB : (s + 1) * HUB, :]
    for j in list(range(1, row_count, 2)) + list(range(0, row_count, 2)):
        heads[j] = sums[j].astype(BF16)
        mover.put(heads.at[j], odd_ref.at[j // 2] if j % 2 else even_refs[j // 2])
    back[...] = returns[depth:, :].astype(BF16)
    for k, ref in enumerate(back_refs):
        mover.put(back.at[aligned((group ^ k) * size, size)], ref)
    mover.drain()


def block(index, owners, degrees, self_weight, neighbor_weight, features, values, hub, cut, cotangent, heads, pieces, passed):
    count, width = features.shape
    tiles = values.shape[0]
    row_count, groups = len(heads) + 1, 2 * len(pieces)
    half = row_count // 2
    piece = cut.shape[1] // groups
    depth = hub.shape[1] + cut.shape[1]
    flops = 2 * count * width * (2 * hub.shape[1] + 2 * cut.shape[1] + 5 * width)
    near = pltpu.VMEM((count, width), BF16)

    def kernel(*refs):
        block_kernel(row_count, groups, *refs)

    out = call(
        kernel,
        "block",
        (
            index, owners, degrees, self_weight, neighbor_weight,
            features, values, hub, cut, cotangent, *heads, *pieces, *passed,
        ),
        [((count, width), BF16)] * 3
        + [((2 * width, width), BF16), ((half, HUB, width), BF16)]
        + [((HUB, width), BF16)] * half
        + [((piece, width), BF16)] * groups,
        [SCALARS, SCALARS, NEAR] + [ANY] * (7 + len(heads) + groups),
        [ANY] * (5 + half + groups),
        [
            pltpu.VMEM((count, 2 * width), BF16),
            pltpu.VMEM((2 * width, width), BF16),
            pltpu.VMEM(values.shape, BF16),
            pltpu.VMEM((count, depth), BF16),
            near,
            pltpu.VMEM((row_count, HUB, width), BF16),
            pltpu.VMEM((depth, width), BF16),
            pltpu.VMEM((count, width), F32),
            near,
            near,
            near,
            pltpu.VMEM((2 * width, width), BF16),
            pltpu.VMEM((row_count, HUB, width), F32),
            pltpu.VMEM((cut.shape[1], width), BF16),
            pltpu.SemaphoreType.DMA(
                (7 * count // CHUNK + tiles // TILE_STEP + 2 * row_count + 2 * groups + 2,)
            ),
        ],
        flops + 2 * tiles * TILE * TILE * width,
        2 * hub.size + 2 * cut.size + 2 * values.size + 14 * features.size,
    )
    hidden, grad, aggregate, weights, odds = out[:5]
    return hidden, grad, aggregate, weights, odds, out[5 : 5 + half], out[5 + half :]


def local_back_kernel(groups, *refs):
    index_ref, self_ref, rows_ref, values_ref, aggregate_ref, grad_ref = refs[:6]
    piece_refs = refs[6 : 6 + groups]
    out_ref, head_ref, values, aggregate, grad, returned, total, result, sems = refs[6 + groups :]
    size = piece_refs[0].shape[0]
    picks = returned.shape[0]
    group = lax.axis_index("grp")

    mover = Mover(sems)
    parts = split(grad_ref.shape[0], CHUNK)
    first = [mover.get(grad_ref.at[part], grad.at[part]) for part in parts]
    back = [
        mover.get(ref, returned.at[aligned((group ^ k) * size, size)])
        for k, ref in enumerate(piece_refs)
    ]
    coming = [mover.get(aggregate_ref.at[part], aggregate.at[part]) for part in parts]
    steps = split(values_ref.shape[0], TILE_STEP)
    tiles = [mover.get(values_ref.at[part], values.at[part]) for part in steps]
    rows = jnp.concatenate([rows_ref[0, j : j + 1, :] for j in range(groups)], axis=1)
    wait(back)
    for part, copy in zip(parts, first):
        where = lax.broadcasted_iota(jnp.int32, (CHUNK, picks), 0) + part.start
        table = jnp.where(where == rows, 1.0, 0.0).astype(BF16)
        copy.wait()
        total[part, :] = dot(grad[part, :], self_ref[...], COLS) + dot(table, returned[...])
    wait(coming)
    for part, copy in zip(steps, tiles):
        copy.wait()
        for t in range(part.start, part.stop):
            row = aligned(index_ref[0, 0, t] * TILE, TILE)
            col = aligned(index_ref[0, 1, t] * TILE, TILE)
            total[col, :] += dot(values[t], aggregate[row, :], ROWS)
    mover.put(total.at[:HUB], head_ref)
    for part in parts:
        result[part, :] = total[part, :].astype(BF16)
        mover.put(result.at[part], out_ref.at[part])
    mover.drain()


def local_backward(index, self_weight, rows, values, aggregate, grad, pieces):
    tiles = values.shape[0]
    count, width = grad.shape
    groups = len(pieces)
    picks = groups * rows.shape[2]
    near = pltpu.VMEM((count, width), BF16)

    def kernel(*refs):
        local_back_kernel(groups, *refs)

    return call(
        kernel,
        "local_backward",
        (index, self_weight, rows, values, aggregate, grad, *pieces),
        [((count, width), BF16), ((HUB, width), F32)],
        [SCALARS, NEAR, NEAR] + [ANY] * (3 + groups),
        [ANY, ANY],
        [
            pltpu.VMEM(values.shape, BF16),
            near,
            near,
            pltpu.VMEM((picks, width), BF16),
            pltpu.VMEM((count, width), F32),
            near,
            pltpu.SemaphoreType.DMA((3 * count // CHUNK + groups + tiles // TILE_STEP + 1,)),
        ],
        2 * tiles * TILE * TILE * width + 2 * count * width * (width + picks),
        2 * values.size + 8 * grad.size,
    )


def finish_kernel(grad_ref, local_ref, weights_ref, mine_ref, side_ref, *refs):
    head_refs = refs[:-8]
    out_ref, self_ref, neighbor_ref, local, weights, sums, heads, sems = refs[-8:]
    width = weights_ref.shape[1]
    mover = Mover(sems)
    ends = [mine_ref, side_ref.at[0], *head_refs]
    first = [mover.get(local_ref, local)]
    first += [mover.get(ref, heads.at[k]) for k, ref in enumerate(ends)]
    mover.get(weights_ref, weights).wait()
    sums[...] = weights[...].astype(F32)
    mover.put(sums.at[:width], self_ref)
    mover.put(sums.at[width:], neighbor_ref)
    wait(first)
    total = local[...] + jnp.sum(heads[...].astype(F32), axis=0)
    heads[0] = total.astype(BF16)
    mover.put(heads.at[0], out_ref.at[:HUB])
    mover.drain()


def finish(grad, local, weights, mine, side, heads):
    width = grad.shape[1]
    return pl.pallas_call(
        finish_kernel,
        in_specs=[ANY] * (5 + len(heads)),
        out_specs=[ANY] * 3,
        out_shape=[
            jax.ShapeDtypeStruct(grad.shape, BF16),
            jax.ShapeDtypeStruct((width, width), F32),
            jax.ShapeDtypeStruct((width, width), F32),
        ],
        scratch_shapes=[
            pltpu.VMEM((HUB, width), F32),
            pltpu.VMEM((2 * width, width), BF16),
            pltpu.VMEM((2 * width, width), F32),
            pltpu.VMEM((len(heads) + 2, HUB, width), BF16),
            pltpu.SemaphoreType.DMA((len(heads) + 7,)),
        ],
        input_output_aliases={0: 0},
        compiler_params=pltpu.CompilerParams(vmem_limit_bytes=VMEM_LIMIT),
        cost_estimate=pl.CostEstimate(flops=weights.size, bytes_accessed=8 * weights.size, transcendentals=0),
        name="finish",
    )(grad, local, weights, mine, side, *heads)


def trade(value, axis, k):
    return lax.ppermute(value, axis, [(r, r ^ k) for r in range(lax.axis_size(axis))])


def on_device(
    features,
    cotangent,
    self_weight,
    neighbor_weight,
    tile_values,
    tile_index,
    hub_adjacency,
    hub_owner,
    send_rows,
    cut_adjacency,
    degrees,
):
    count, width = features.shape
    groups = lax.axis_size("grp")
    row_count = lax.axis_size("row")
    everyone = ("grp", "row")
    values = tile_values[0]
    index = tile_index.transpose(0, 2, 1)
    degrees = degrees.reshape(count // TILE, TILE)

    head, odds, *pieces = pick_rows(send_rows, features)
    evens = [head] + [trade(head, "row", k) for k in range(2, row_count, 2)]
    odds, evens[-1] = lax.optimization_barrier((trade(odds, "grp", 1), evens[-1]))
    heads = [x for even in evens for x in (even, trade(even, "row", 1))][1:]
    pieces = [pieces[0]] + [trade(pieces[k], "grp", 2 * k) for k in range(1, groups // 2)]
    passed = [odds] + [trade(odds, "grp", 2 * k) for k in range(1, groups // 2)]
    hidden, grad, aggregate, weights, odds, evens, pieces = block(
        index, hub_owner, degrees, self_weight, neighbor_weight, features, values,
        hub_adjacency, cut_adjacency, cotangent, heads, pieces, passed,
    )
    parts = weights.reshape(groups * row_count, -1, width)
    parts = lax.all_to_all(parts, everyone, split_axis=0, concat_axis=0, tiled=True)
    odds = trade(odds, "row", 1)
    heads = [
        trade((even.astype(F32) + odds[j + 1].astype(F32)).astype(BF16), "row", 2 * j + 2)
        for j, even in enumerate(evens[1:])
    ]
    pieces = [pieces[0]] + [trade(pieces[k], "grp", k) for k in range(1, groups)]
    parts, pieces = lax.optimization_barrier((parts, pieces))
    sums = jnp.sum(parts.astype(F32), axis=0).astype(BF16)
    sums = jnp.broadcast_to(sums[None], parts.shape)
    sums = lax.all_to_all(sums, everyone, split_axis=0, concat_axis=0, tiled=True)
    grad_features, head = local_backward(
        index, self_weight, send_rows, values, aggregate, grad, pieces
    )
    grad_features, grad_self, grad_neighbor = finish(
        grad_features, head, sums.reshape(2 * width, width), evens[0], odds, heads
    )
    return hidden, grad_features, grad_self, grad_neighbor


def solution(mesh):
    nodes = P(("grp", "row"), None)
    in_specs = (
        nodes,
        nodes,
        P(),
        P(),
        P(("grp", "row"), None, None, None),
        P(("grp", "row"), None, None),
        nodes,
        P("grp", None),
        P(("grp", "row"), None, None),
        nodes,
        P(("grp", "row")),
    )
    out_specs = (nodes, nodes, P(), P())
    return jax.shard_map(
        on_device, mesh=mesh, in_specs=in_specs, out_specs=out_specs, check_vma=False
    )
```

```python
import jax
import jax.numpy as jnp
from jax import lax
from jax.experimental import pallas as pl
from jax.experimental.pallas import tpu as pltpu
from jax.sharding import PartitionSpec as P

TILE = 128
HUB = 128
CHUNK = 1024
TILE_STEP = 32
VMEM_LIMIT = 62 * 2**20
ROWS = (((0,), (0,)), ((), ()))
COLS = (((1,), (1,)), ((), ()))
F32 = jnp.float32
BF16 = jnp.bfloat16
ANY = pl.BlockSpec(memory_space=pl.ANY)
NEAR = pl.BlockSpec(memory_space=pltpu.VMEM)
SCALARS = pl.BlockSpec(memory_space=pltpu.SMEM)


def call(kernel, name, ins, outs, in_specs, out_specs, scratch, flops, moved):
    return pl.pallas_call(
        kernel,
        in_specs=in_specs,
        out_specs=out_specs,
        out_shape=[jax.ShapeDtypeStruct(shape, dtype) for shape, dtype in outs],
        scratch_shapes=scratch,
        compiler_params=pltpu.CompilerParams(vmem_limit_bytes=VMEM_LIMIT),
        cost_estimate=pl.CostEstimate(flops=flops, bytes_accessed=moved, transcendentals=0),
        name=name,
    )(*ins)


def dot(a, b, dims=(((1,), (0,)), ((), ()))):
    return lax.dot_general(a, b, dims, preferred_element_type=F32)


def aligned(start, size):
    return pl.ds(pl.multiple_of(start, size), size)


class Mover:
    def __init__(self, sems):
        self.sems, self.used, self.out = sems, 0, []

    def get(self, source, target):
        copy = pltpu.make_async_copy(source, target, self.sems.at[self.used])
        self.used += 1
        copy.start()
        return copy

    def put(self, source, target):
        self.out.append(self.get(source, target))

    def drain(self):
        wait(self.out)


def wait(started):
    for copy in started:
        copy.wait()


def split(count, step):
    return [slice(i, i + step) for i in range(0, count, step)]


def pick_kernel(far_rows_ref, features_ref, *rest):
    out_refs, (rows_ref, features, picked, sems) = rest[:-4], rest[-4:]
    groups, cut = rows_ref.shape[1:]
    count = features_ref.shape[0]
    group = lax.axis_index("grp")
    mover = Mover(sems)
    parts = split(count, CHUNK)
    lines = mover.get(far_rows_ref, rows_ref)
    coming = [mover.get(features_ref.at[part], features.at[part]) for part in parts]
    lines.wait()
    across = lax.broadcasted_iota(jnp.int32, (cut, cut), 0)
    along = lax.broadcasted_iota(jnp.int32, (cut, cut), 1)
    columns = []
    for j in range(groups):
        line = jnp.broadcast_to(rows_ref[0, j : j + 1, :].astype(F32), (cut, cut))
        columns.append(jnp.sum(jnp.where(across == along, line, 0.0), axis=1, keepdims=True))
    column = jnp.concatenate(columns, axis=0).astype(jnp.int32)
    where = lax.broadcasted_iota(jnp.int32, (groups * cut, count), 1)
    table = jnp.where(where == column, 1.0, 0.0).astype(BF16)
    wait(coming)
    picked[...] = dot(table, features[...]).astype(BF16)
    odd_ref, even_refs = out_refs[0], out_refs[1:]
    for k in range(groups):
        ref = odd_ref.at[k // 2] if k % 2 else even_refs[k // 2]
        mover.put(picked.at[aligned((group ^ k) * cut, cut)], ref)
    mover.drain()


def pick_rows(rows, features):
    _, groups, cut = rows.shape
    count, width = features.shape
    return call(
        pick_kernel,
        "pick_rows",
        (rows, features),
        [((groups // 2, cut, width), BF16)]
        + [((cut, width), BF16)] * (groups // 2),
        [ANY, ANY],
        [ANY] * (1 + groups // 2),
        [
            pltpu.VMEM(rows.shape, jnp.int32),
            pltpu.VMEM((count, width), BF16),
            pltpu.VMEM((groups * cut, width), BF16),
            pltpu.SemaphoreType.DMA((1 + groups + count // CHUNK,)),
        ],
        2 * groups * cut * count * width,
        2 * count * width,
    )


def scale_of(degrees_ref, part, width):
    lines = lax.rsqrt(degrees_ref[part.start // TILE : part.stop // TILE, :].astype(F32))
    blocks = [
        jnp.broadcast_to(lines[j : j + 1, :], (TILE, TILE)).T for j in range(lines.shape[0])
    ]
    return jnp.concatenate([jnp.concatenate(blocks, axis=0)] * (width // TILE), axis=1)


def block_kernel(row_count, groups, *refs):
    far_index_ref, far_owner_ref, far_degrees_ref, self_ref, neighbor_ref = refs[:5]
    features_ref, values_ref, hub_ref, cut_ref, cotangent_ref = refs[5:10]
    head_refs = refs[10 : 9 + row_count]
    piece_refs = refs[9 + row_count : 9 + row_count + groups]
    outs = refs[9 + row_count + groups : -18]
    hidden_ref, grad_ref, aggregate_ref, weights_ref, odd_ref = outs[:5]
    even_refs, back_refs = outs[5 : 5 + row_count // 2], outs[5 + row_count // 2 :]
    index_ref, owner_ref, degrees_ref = refs[-18:-15]
    pair, stack, values, edges, cotangent, heads, panels = refs[-15:-8]
    total, hidden, grad, aggregate, weights, sums, back, sems = refs[-8:]
    count, width = features_ref.shape
    depth = hub_ref.shape[1]
    sections = depth // HUB
    size = piece_refs[0].shape[0]
    group, place = lax.axis_index("grp"), lax.axis_index("row")

    mover = Mover(sems)
    parts = split(count, CHUNK)
    steps = split(values_ref.shape[0], TILE_STEP)
    rows = [mover.get(far_index_ref, index_ref), mover.get(far_owner_ref, owner_ref)]
    rows += [mover.get(far_degrees_ref, degrees_ref)]
    rows += [mover.get(features_ref, pair.at[:, :width])]
    tiles = [mover.get(values_ref.at[part], values.at[part]) for part in steps]
    first = [mover.get(ref, heads.at[k + 1]) for k, ref in enumerate(head_refs)]
    for k in range(groups):
        ref = piece_refs[groups // 2 + k // 2].at[k // 2] if k % 2 else piece_refs[k // 2]
        first.append(mover.get(ref, panels.at[aligned(depth + (group ^ k) * size, size)]))
    first += [
        mover.get(self_ref, stack.at[:width]), mover.get(neighbor_ref, stack.at[width:])
    ]
    coming = []
    for part in parts:
        coming.append([
            mover.get(hub_ref.at[part], edges.at[part, :depth]),
            mover.get(cut_ref.at[part], edges.at[part, depth:]),
            mover.get(cotangent_ref.at[part], cotangent.at[part]),
        ])

    total[...] = jnp.zeros_like(total)
    wait(rows)
    for part, copy in zip(steps, tiles):
        copy.wait()
        for t in range(part.start, part.stop):
            row = aligned(index_ref[0, 0, t] * TILE, TILE)
            col = aligned(index_ref[0, 1, t] * TILE, TILE)
            total[row, :] += dot(values[t], pair[col, :width])

    wait(first)
    heads[0] = pair[:HUB, :width]
    for s in range(sections):
        panels[s * HUB : (s + 1) * HUB, :] = heads[owner_ref[0, s] ^ place]
    neighbor = stack[width:, :]
    root, bend = 0.7978845608028654, 0.044715
    for part, copies in zip(parts, coming):
        wait(copies)
        scale = scale_of(degrees_ref, part, width)
        summed = total[part, :] + dot(edges[part, :], panels[...])
        pair[part, width:] = (summed * scale).astype(BF16)
        before = dot(pair[part, :], stack[...])
        slope = (root * bend) * (before * before) + root
        wave = jnp.tanh(before * slope)
        half = 0.5 * wave + 0.5
        hidden[part, :] = (before * half).astype(BF16)
        rise = half + (before * (1.5 * slope - root)) * (1.0 - wave * wave)
        new = (cotangent[part, :].astype(F32) * rise).astype(BF16)
        grad[part, :] = new
        aggregate[part, :] = (dot(new, neighbor, COLS) * scale).astype(BF16)
        mover.put(hidden.at[part], hidden_ref.at[part])
        mover.put(grad.at[part], grad_ref.at[part])
        mover.put(aggregate.at[part], aggregate_ref.at[part])
    weights[...] = dot(pair[...], grad[...], ROWS).astype(BF16)
    mover.put(weights, weights_ref)
    sums[...] = jnp.zeros_like(sums)
    returns = dot(edges[...], aggregate[...], ROWS)
    for s in range(sections):
        sums[owner_ref[0, s] ^ place] += returns[s * HUB : (s + 1) * HUB, :]
    for j in list(range(1, row_count, 2)) + list(range(0, row_count, 2)):
        heads[j] = sums[j].astype(BF16)
        mover.put(heads.at[j], odd_ref.at[j // 2] if j % 2 else even_refs[j // 2])
    back[...] = returns[depth:, :].astype(BF16)
    for k, ref in enumerate(back_refs):
        mover.put(back.at[aligned((group ^ k) * size, size)], ref)
    mover.drain()


def block(index, owners, degrees, self_weight, neighbor_weight, features, values, hub, cut, cotangent, heads, pieces, passed):
    count, width = features.shape
    tiles = values.shape[0]
    row_count, groups = len(heads) + 1, 2 * len(pieces)
    half = row_count // 2
    piece = cut.shape[1] // groups
    depth = hub.shape[1] + cut.shape[1]
    flops = 2 * count * width * (2 * hub.shape[1] + 2 * cut.shape[1] + 5 * width)
    near = pltpu.VMEM((count, width), BF16)

    def kernel(*refs):
        block_kernel(row_count, groups, *refs)

    out = call(
        kernel,
        "block",
        (
            index, owners, degrees, self_weight, neighbor_weight,
            features, values, hub, cut, cotangent, *heads, *pieces, *passed,
        ),
        [((count, width), BF16)] * 3
        + [((2 * width, width), BF16), ((half, HUB, width), BF16)]
        + [((HUB, width), BF16)] * half
        + [((piece, width), BF16)] * groups,
        [ANY] * (10 + len(heads) + groups),
        [ANY] * (5 + half + groups),
        [
            pltpu.SMEM(index.shape, jnp.int32),
            pltpu.SMEM(owners.shape, jnp.int32),
            pltpu.VMEM(degrees.shape, jnp.int32),
            pltpu.VMEM((count, 2 * width), BF16),
            pltpu.VMEM((2 * width, width), BF16),
            pltpu.VMEM(values.shape, BF16),
            pltpu.VMEM((count, depth), BF16),
            near,
            pltpu.VMEM((row_count, HUB, width), BF16),
            pltpu.VMEM((depth, width), BF16),
            pltpu.VMEM((count, width), F32),
            near,
            near,
            near,
            pltpu.VMEM((2 * width, width), BF16),
            pltpu.VMEM((row_count, HUB, width), F32),
            pltpu.VMEM((cut.shape[1], width), BF16),
            pltpu.SemaphoreType.DMA(
                (7 * count // CHUNK + tiles // TILE_STEP + 2 * row_count + 2 * groups + 5,)
            ),
        ],
        flops + 2 * tiles * TILE * TILE * width,
        2 * hub.size + 2 * cut.size + 2 * values.size + 14 * features.size,
    )
    hidden, grad, aggregate, weights, odds = out[:5]
    return hidden, grad, aggregate, weights, odds, out[5 : 5 + half], out[5 + half :]


def local_back_kernel(groups, *refs):
    far_index_ref, far_self_ref, far_rows_ref, values_ref, aggregate_ref, grad_ref = refs[:6]
    piece_refs = refs[6 : 6 + groups]
    out_ref, head_ref, index_ref, self_ref, rows_ref, values, aggregate, grad = refs[6 + groups : -4]
    returned, total, result, sems = refs[-4:]
    size = piece_refs[0].shape[0]
    picks = returned.shape[0]
    group = lax.axis_index("grp")

    mover = Mover(sems)
    parts = split(grad_ref.shape[0], CHUNK)
    back = [mover.get(far_rows_ref, rows_ref), mover.get(far_self_ref, self_ref)]
    back += [mover.get(far_index_ref, index_ref)]
    first = [mover.get(grad_ref.at[part], grad.at[part]) for part in parts]
    back += [
        mover.get(ref, returned.at[aligned((group ^ k) * size, size)])
        for k, ref in enumerate(piece_refs)
    ]
    coming = [mover.get(aggregate_ref.at[part], aggregate.at[part]) for part in parts]
    steps = split(values_ref.shape[0], TILE_STEP)
    tiles = [mover.get(values_ref.at[part], values.at[part]) for part in steps]
    wait(back)
    rows = jnp.concatenate([rows_ref[0, j : j + 1, :] for j in range(groups)], axis=1)
    for part, copy in zip(parts, first):
        where = lax.broadcasted_iota(jnp.int32, (CHUNK, picks), 0) + part.start
        table = jnp.where(where == rows, 1.0, 0.0).astype(BF16)
        copy.wait()
        total[part, :] = dot(grad[part, :], self_ref[...], COLS) + dot(table, returned[...])
    wait(coming)
    for part, copy in zip(steps, tiles):
        copy.wait()
        for t in range(part.start, part.stop):
            row = aligned(index_ref[0, 0, t] * TILE, TILE)
            col = aligned(index_ref[0, 1, t] * TILE, TILE)
            total[col, :] += dot(values[t], aggregate[row, :], ROWS)
    mover.put(total.at[:HUB], head_ref)
    for part in parts:
        result[part, :] = total[part, :].astype(BF16)
        mover.put(result.at[part], out_ref.at[part])
    mover.drain()


def local_backward(index, self_weight, rows, values, aggregate, grad, pieces):
    tiles = values.shape[0]
    count, width = grad.shape
    groups = len(pieces)
    picks = groups * rows.shape[2]
    near = pltpu.VMEM((count, width), BF16)

    def kernel(*refs):
        local_back_kernel(groups, *refs)

    return call(
        kernel,
        "local_backward",
        (index, self_weight, rows, values, aggregate, grad, *pieces),
        [((count, width), BF16), ((HUB, width), F32)],
        [ANY] * (6 + groups),
        [ANY, ANY],
        [
            pltpu.SMEM(index.shape, jnp.int32),
            pltpu.VMEM(self_weight.shape, BF16),
            pltpu.VMEM(rows.shape, jnp.int32),
            pltpu.VMEM(values.shape, BF16),
            near,
            near,
            pltpu.VMEM((picks, width), BF16),
            pltpu.VMEM((count, width), F32),
            near,
            pltpu.SemaphoreType.DMA((3 * count // CHUNK + groups + tiles // TILE_STEP + 4,)),
        ],
        2 * tiles * TILE * TILE * width + 2 * count * width * (width + picks),
        2 * values.size + 8 * grad.size,
    )


def finish_kernel(grad_ref, local_ref, weights_ref, mine_ref, side_ref, *refs):
    head_refs = refs[:-8]
    out_ref, self_ref, neighbor_ref, local, weights, sums, heads, sems = refs[-8:]
    width = weights_ref.shape[1]
    mover = Mover(sems)
    ends = [mine_ref, side_ref.at[0], *head_refs]
    first = [mover.get(local_ref, local)]
    first += [mover.get(ref, heads.at[k]) for k, ref in enumerate(ends)]
    mover.get(weights_ref, weights).wait()
    sums[...] = weights[...].astype(F32)
    mover.put(sums.at[:width], self_ref)
    mover.put(sums.at[width:], neighbor_ref)
    wait(first)
    total = local[...] + jnp.sum(heads[...].astype(F32), axis=0)
    heads[0] = total.astype(BF16)
    mover.put(heads.at[0], out_ref.at[:HUB])
    mover.drain()


def finish(grad, local, weights, mine, side, heads):
    width = grad.shape[1]
    return pl.pallas_call(
        finish_kernel,
        in_specs=[ANY] * (5 + len(heads)),
        out_specs=[ANY] * 3,
        out_shape=[
            jax.ShapeDtypeStruct(grad.shape, BF16),
            jax.ShapeDtypeStruct((width, width), F32),
            jax.ShapeDtypeStruct((width, width), F32),
        ],
        scratch_shapes=[
            pltpu.VMEM((HUB, width), F32),
            pltpu.VMEM((2 * width, width), BF16),
            pltpu.VMEM((2 * width, width), F32),
            pltpu.VMEM((len(heads) + 2, HUB, width), BF16),
            pltpu.SemaphoreType.DMA((len(heads) + 7,)),
        ],
        input_output_aliases={0: 0},
        compiler_params=pltpu.CompilerParams(vmem_limit_bytes=VMEM_LIMIT),
        cost_estimate=pl.CostEstimate(flops=weights.size, bytes_accessed=8 * weights.size, transcendentals=0),
        name="finish",
    )(grad, local, weights, mine, side, *heads)


def trade(value, axis, k):
    return lax.ppermute(value, axis, [(r, r ^ k) for r in range(lax.axis_size(axis))])


def on_device(
    features,
    cotangent,
    self_weight,
    neighbor_weight,
    tile_values,
    tile_index,
    hub_adjacency,
    hub_owner,
    send_rows,
    cut_adjacency,
    degrees,
):
    count, width = features.shape
    groups = lax.axis_size("grp")
    row_count = lax.axis_size("row")
    everyone = ("grp", "row")
    values = tile_values[0]
    index = tile_index.transpose(0, 2, 1)
    degrees = degrees.reshape(count // TILE, TILE)

    head = features[:HUB]
    evens = [head] + [trade(head, "row", k) for k in range(2, row_count, 2)]
    rows, evens[1] = lax.optimization_barrier((send_rows, evens[1]))
    odds, *pieces = pick_rows(rows, features)
    pieces = [pieces[0]] + [trade(pieces[k], "grp", 2 * k) for k in range(1, groups // 2)]
    odds = trade(odds, "grp", 1)
    odds, pieces = lax.optimization_barrier((odds, pieces))
    heads = [x for even in evens for x in (even, trade(even, "row", 1))][1:]
    passed = [odds] + [trade(odds, "grp", 2 * k) for k in range(1, groups // 2)]
    hidden, grad, aggregate, weights, odds, evens, pieces = block(
        index, hub_owner, degrees, self_weight, neighbor_weight, features, values,
        hub_adjacency, cut_adjacency, cotangent, heads, pieces, passed,
    )
    odds = trade(odds, "row", 1)
    parts = weights.reshape(groups * row_count, -1, width)
    parts = lax.all_to_all(parts, everyone, split_axis=0, concat_axis=0, tiled=True)
    heads = [
        trade((even.astype(F32) + odds[j + 1].astype(F32)).astype(BF16), "row", 2 * j + 2)
        for j, even in enumerate(evens[1:])
    ]
    pieces = [pieces[0]] + [trade(pieces[k], "grp", k) for k in range(1, groups)]
    parts, pieces = lax.optimization_barrier((parts, pieces))
    sums = jnp.sum(parts.astype(F32), axis=0).astype(BF16)
    sums = jnp.broadcast_to(sums[None], parts.shape)
    sums = lax.all_to_all(sums, everyone, split_axis=0, concat_axis=0, tiled=True)
    grad_features, head = local_backward(
        index, self_weight, send_rows, values, aggregate, grad, pieces
    )
    grad_features, grad_self, grad_neighbor = finish(
        grad_features, head, sums.reshape(2 * width, width), evens[0], odds, heads
    )
    return hidden, grad_features, grad_self, grad_neighbor


def solution(mesh):
    nodes = P(("grp", "row"), None)
    in_specs = (
        nodes,
        nodes,
        P(),
        P(),
        P(("grp", "row"), None, None, None),
        P(("grp", "row"), None, None),
        nodes,
        P("grp", None),
        P(("grp", "row"), None, None),
        nodes,
        P(("grp", "row")),
    )
    out_specs = (nodes, nodes, P(), P())
    return jax.shard_map(
        on_device, mesh=mesh, in_specs=in_specs, out_specs=out_specs, check_vma=False
    )
```

```python
import jax
import jax.numpy as jnp
from jax import lax
from jax.experimental import pallas as pl
from jax.experimental.pallas import tpu as pltpu
from jax.sharding import PartitionSpec as P

TILE = 128
HUB = 128
CHUNK = 1024
TILE_STEP = 32
VMEM_LIMIT = 62 * 2**20
ROWS = (((0,), (0,)), ((), ()))
COLS = (((1,), (1,)), ((), ()))
F32 = jnp.float32
BF16 = jnp.bfloat16
ANY = pl.BlockSpec(memory_space=pl.ANY)
NEAR = pl.BlockSpec(memory_space=pltpu.VMEM)
SCALARS = pl.BlockSpec(memory_space=pltpu.SMEM)


def call(kernel, name, ins, outs, in_specs, out_specs, scratch, flops, moved):
    return pl.pallas_call(
        kernel,
        in_specs=in_specs,
        out_specs=out_specs,
        out_shape=[jax.ShapeDtypeStruct(shape, dtype) for shape, dtype in outs],
        scratch_shapes=scratch,
        compiler_params=pltpu.CompilerParams(vmem_limit_bytes=VMEM_LIMIT),
        cost_estimate=pl.CostEstimate(flops=flops, bytes_accessed=moved, transcendentals=0),
        name=name,
    )(*ins)


def dot(a, b, dims=(((1,), (0,)), ((), ()))):
    return lax.dot_general(a, b, dims, preferred_element_type=F32)


def aligned(start, size):
    return pl.ds(pl.multiple_of(start, size), size)


class Mover:
    def __init__(self, sems):
        self.sems, self.used, self.out = sems, 0, []

    def get(self, source, target):
        copy = pltpu.make_async_copy(source, target, self.sems.at[self.used])
        self.used += 1
        copy.start()
        return copy

    def put(self, source, target):
        self.out.append(self.get(source, target))

    def drain(self):
        wait(self.out)


def wait(started):
    for copy in started:
        copy.wait()


def split(count, step):
    return [slice(i, i + step) for i in range(0, count, step)]


def pick_kernel(far_rows_ref, features_ref, *rest):
    out_refs, (rows_ref, features, picked, sems) = rest[:-4], rest[-4:]
    groups, cut = rows_ref.shape[1:]
    count = features_ref.shape[0]
    group = lax.axis_index("grp")
    mover = Mover(sems)
    parts = split(count, CHUNK)
    lines = mover.get(far_rows_ref, rows_ref)
    coming = [mover.get(features_ref.at[part], features.at[part]) for part in parts]
    lines.wait()
    across = lax.broadcasted_iota(jnp.int32, (cut, cut), 0)
    along = lax.broadcasted_iota(jnp.int32, (cut, cut), 1)
    columns = []
    for j in range(groups):
        line = jnp.broadcast_to(rows_ref[0, j : j + 1, :].astype(F32), (cut, cut))
        columns.append(jnp.sum(jnp.where(across == along, line, 0.0), axis=1, keepdims=True))
    column = jnp.concatenate(columns, axis=0).astype(jnp.int32)
    where = lax.broadcasted_iota(jnp.int32, (groups * cut, count), 1)
    table = jnp.where(where == column, 1.0, 0.0).astype(BF16)
    wait(coming)
    picked[...] = dot(table, features[...]).astype(BF16)
    odd_ref, even_refs = out_refs[0], out_refs[1:]
    for k in range(groups):
        ref = odd_ref.at[k // 2] if k % 2 else even_refs[k // 2]
        mover.put(picked.at[aligned((group ^ k) * cut, cut)], ref)
    mover.drain()


def pick_rows(rows, features):
    _, groups, cut = rows.shape
    count, width = features.shape
    return call(
        pick_kernel,
        "pick_rows",
        (rows, features),
        [((groups // 2, cut, width), BF16)]
        + [((cut, width), BF16)] * (groups // 2),
        [ANY, ANY],
        [ANY] * (1 + groups // 2),
        [
            pltpu.VMEM(rows.shape, jnp.int32),
            pltpu.VMEM((count, width), BF16),
            pltpu.VMEM((groups * cut, width), BF16),
            pltpu.SemaphoreType.DMA((1 + groups + count // CHUNK,)),
        ],
        2 * groups * cut * count * width,
        2 * count * width,
    )


def scale_of(degrees_ref, part, width):
    lines = lax.rsqrt(degrees_ref[part.start // TILE : part.stop // TILE, :].astype(F32))
    blocks = [
        jnp.broadcast_to(lines[j : j + 1, :], (TILE, TILE)).T for j in range(lines.shape[0])
    ]
    return jnp.concatenate([jnp.concatenate(blocks, axis=0)] * (width // TILE), axis=1)


def block_kernel(row_count, groups, *refs):
    far_index_ref, far_owner_ref, far_degrees_ref, self_ref, neighbor_ref = refs[:5]
    features_ref, values_ref, hub_ref, cut_ref, cotangent_ref = refs[5:10]
    head_refs = refs[10 : 9 + row_count]
    piece_refs = refs[9 + row_count : 9 + row_count + groups]
    outs = refs[9 + row_count + groups : -18]
    hidden_ref, grad_ref, aggregate_ref, weights_ref, odd_ref = outs[:5]
    even_refs, back_refs = outs[5 : 5 + row_count // 2], outs[5 + row_count // 2 :]
    index_ref, owner_ref, degrees_ref = refs[-18:-15]
    pair, stack, values, edges, cotangent, heads, panels = refs[-15:-8]
    total, hidden, grad, aggregate, weights, sums, back, sems = refs[-8:]
    count, width = features_ref.shape
    depth = hub_ref.shape[1]
    sections = depth // HUB
    size = piece_refs[0].shape[0]
    group, place = lax.axis_index("grp"), lax.axis_index("row")

    mover = Mover(sems)
    early = count * 3 // 8
    parts = [slice(0, early), slice(early, count)]
    steps = split(values_ref.shape[0], TILE_STEP)
    rows = [mover.get(far_index_ref, index_ref), mover.get(far_owner_ref, owner_ref)]
    rows += [mover.get(far_degrees_ref, degrees_ref)]
    rows += [mover.get(features_ref, pair.at[:, :width])]
    tiles = [mover.get(values_ref.at[part], values.at[part]) for part in steps]
    first = [mover.get(ref, heads.at[k + 1]) for k, ref in enumerate(head_refs)]
    for k in range(groups):
        ref = piece_refs[groups // 2 + k // 2].at[k // 2] if k % 2 else piece_refs[k // 2]
        first.append(mover.get(ref, panels.at[aligned(depth + (group ^ k) * size, size)]))
    first += [
        mover.get(self_ref, stack.at[:width]), mover.get(neighbor_ref, stack.at[width:])
    ]
    coming = []
    for part in parts:
        coming.append([
            mover.get(hub_ref.at[part], edges.at[part, :depth]),
            mover.get(cut_ref.at[part], edges.at[part, depth:]),
            mover.get(cotangent_ref.at[part], cotangent.at[part]),
        ])

    total[...] = jnp.zeros_like(total)
    wait(rows)
    for part, copy in zip(steps, tiles):
        copy.wait()
        for t in range(part.start, part.stop):
            row = aligned(index_ref[0, 0, t] * TILE, TILE)
            col = aligned(index_ref[0, 1, t] * TILE, TILE)
            total[row, :] += dot(values[t], pair[col, :width])

    wait(first)
    heads[0] = pair[:HUB, :width]
    for s in range(sections):
        panels[s * HUB : (s + 1) * HUB, :] = heads[owner_ref[0, s] ^ place]
    neighbor = stack[width:, :]
    root, bend = 0.7978845608028654, 0.044715
    for part, copies in zip(parts, coming):
        wait(copies)
        scale = scale_of(degrees_ref, part, width)
        summed = total[part, :] + dot(edges[part, :], panels[...])
        pair[part, width:] = (summed * scale).astype(BF16)
        before = dot(pair[part, :], stack[...])
        slope = (root * bend) * (before * before) + root
        wave = jnp.tanh(before * slope)
        half = 0.5 * wave + 0.5
        hidden[part, :] = (before * half).astype(BF16)
        rise = half + (before * (1.5 * slope - root)) * (1.0 - wave * wave)
        new = (cotangent[part, :].astype(F32) * rise).astype(BF16)
        grad[part, :] = new
        aggregate[part, :] = (dot(new, neighbor, COLS) * scale).astype(BF16)
        mover.put(hidden.at[part], hidden_ref.at[part])
        mover.put(grad.at[part], grad_ref.at[part])
        mover.put(aggregate.at[part], aggregate_ref.at[part])
    weights[...] = dot(pair[...], grad[...], ROWS).astype(BF16)
    mover.put(weights, weights_ref)
    sums[...] = jnp.zeros_like(sums)
    returns = dot(edges[...], aggregate[...], ROWS)
    for s in range(sections):
        sums[owner_ref[0, s] ^ place] += returns[s * HUB : (s + 1) * HUB, :]
    for j in list(range(1, row_count, 2)) + list(range(0, row_count, 2)):
        heads[j] = sums[j].astype(BF16)
        mover.put(heads.at[j], odd_ref.at[j // 2] if j % 2 else even_refs[j // 2])
    back[...] = returns[depth:, :].astype(BF16)
    for k, ref in enumerate(back_refs):
        mover.put(back.at[aligned((group ^ k) * size, size)], ref)
    mover.drain()


def block(index, owners, degrees, self_weight, neighbor_weight, features, values, hub, cut, cotangent, heads, pieces, passed):
    count, width = features.shape
    tiles = values.shape[0]
    row_count, groups = len(heads) + 1, 2 * len(pieces)
    half = row_count // 2
    piece = cut.shape[1] // groups
    depth = hub.shape[1] + cut.shape[1]
    flops = 2 * count * width * (2 * hub.shape[1] + 2 * cut.shape[1] + 5 * width)
    near = pltpu.VMEM((count, width), BF16)

    def kernel(*refs):
        block_kernel(row_count, groups, *refs)

    out = call(
        kernel,
        "block",
        (
            index, owners, degrees, self_weight, neighbor_weight,
            features, values, hub, cut, cotangent, *heads, *pieces, *passed,
        ),
        [((count, width), BF16)] * 3
        + [((2 * width, width), BF16), ((half, HUB, width), BF16)]
        + [((HUB, width), BF16)] * half
        + [((piece, width), BF16)] * groups,
        [ANY] * (10 + len(heads) + groups),
        [ANY] * (5 + half + groups),
        [
            pltpu.SMEM(index.shape, jnp.int32),
            pltpu.SMEM(owners.shape, jnp.int32),
            pltpu.VMEM(degrees.shape, jnp.int32),
            pltpu.VMEM((count, 2 * width), BF16),
            pltpu.VMEM((2 * width, width), BF16),
            pltpu.VMEM(values.shape, BF16),
            pltpu.VMEM((count, depth), BF16),
            near,
            pltpu.VMEM((row_count, HUB, width), BF16),
            pltpu.VMEM((depth, width), BF16),
            pltpu.VMEM((count, width), F32),
            near,
            near,
            near,
            pltpu.VMEM((2 * width, width), BF16),
            pltpu.VMEM((row_count, HUB, width), F32),
            pltpu.VMEM((cut.shape[1], width), BF16),
            pltpu.SemaphoreType.DMA(
                (14 + tiles // TILE_STEP + 2 * row_count + 2 * groups + 5,)
            ),
        ],
        flops + 2 * tiles * TILE * TILE * width,
        2 * hub.size + 2 * cut.size + 2 * values.size + 14 * features.size,
    )
    hidden, grad, aggregate, weights, odds = out[:5]
    return hidden, grad, aggregate, weights, odds, out[5 : 5 + half], out[5 + half :]


def local_back_kernel(groups, *refs):
    far_index_ref, far_self_ref, far_rows_ref, values_ref, aggregate_ref, grad_ref = refs[:6]
    piece_refs = refs[6 : 6 + groups]
    out_ref, head_ref, index_ref, self_ref, rows_ref, values, aggregate, grad = refs[6 + groups : -4]
    returned, total, result, sems = refs[-4:]
    size = piece_refs[0].shape[0]
    picks = returned.shape[0]
    group = lax.axis_index("grp")

    mover = Mover(sems)
    parts = split(grad_ref.shape[0], CHUNK)
    back = [mover.get(far_rows_ref, rows_ref), mover.get(far_self_ref, self_ref)]
    back += [mover.get(far_index_ref, index_ref)]
    first = [mover.get(grad_ref.at[part], grad.at[part]) for part in parts]
    back += [
        mover.get(ref, returned.at[aligned((group ^ k) * size, size)])
        for k, ref in enumerate(piece_refs)
    ]
    coming = [mover.get(aggregate_ref.at[part], aggregate.at[part]) for part in parts]
    steps = split(values_ref.shape[0], TILE_STEP)
    tiles = [mover.get(values_ref.at[part], values.at[part]) for part in steps]
    wait(back)
    rows = jnp.concatenate([rows_ref[0, j : j + 1, :] for j in range(groups)], axis=1)
    for part, copy in zip(parts, first):
        where = lax.broadcasted_iota(jnp.int32, (CHUNK, picks), 0) + part.start
        table = jnp.where(where == rows, 1.0, 0.0).astype(BF16)
        copy.wait()
        total[part, :] = dot(grad[part, :], self_ref[...], COLS) + dot(table, returned[...])
    wait(coming)
    for part, copy in zip(steps, tiles):
        copy.wait()
        for t in range(part.start, part.stop):
            row = aligned(index_ref[0, 0, t] * TILE, TILE)
            col = aligned(index_ref[0, 1, t] * TILE, TILE)
            total[col, :] += dot(values[t], aggregate[row, :], ROWS)
    mover.put(total.at[:HUB], head_ref)
    for part in parts:
        result[part, :] = total[part, :].astype(BF16)
        mover.put(result.at[part], out_ref.at[part])
    mover.drain()


def local_backward(index, self_weight, rows, values, aggregate, grad, pieces):
    tiles = values.shape[0]
    count, width = grad.shape
    groups = len(pieces)
    picks = groups * rows.shape[2]
    near = pltpu.VMEM((count, width), BF16)

    def kernel(*refs):
        local_back_kernel(groups, *refs)

    return call(
        kernel,
        "local_backward",
        (index, self_weight, rows, values, aggregate, grad, *pieces),
        [((count, width), BF16), ((HUB, width), F32)],
        [ANY] * (6 + groups),
        [ANY, ANY],
        [
            pltpu.SMEM(index.shape, jnp.int32),
            pltpu.VMEM(self_weight.shape, BF16),
            pltpu.VMEM(rows.shape, jnp.int32),
            pltpu.VMEM(values.shape, BF16),
            near,
            near,
            pltpu.VMEM((picks, width), BF16),
            pltpu.VMEM((count, width), F32),
            near,
            pltpu.SemaphoreType.DMA((3 * count // CHUNK + groups + tiles // TILE_STEP + 4,)),
        ],
        2 * tiles * TILE * TILE * width + 2 * count * width * (width + picks),
        2 * values.size + 8 * grad.size,
    )


def finish_kernel(grad_ref, local_ref, weights_ref, mine_ref, side_ref, *refs):
    head_refs = refs[:-8]
    out_ref, self_ref, neighbor_ref, local, weights, sums, heads, sems = refs[-8:]
    width = weights_ref.shape[1]
    mover = Mover(sems)
    ends = [mine_ref, side_ref.at[0], *head_refs]
    first = [mover.get(local_ref, local)]
    first += [mover.get(ref, heads.at[k]) for k, ref in enumerate(ends)]
    mover.get(weights_ref, weights).wait()
    sums[...] = weights[...].astype(F32)
    mover.put(sums.at[:width], self_ref)
    mover.put(sums.at[width:], neighbor_ref)
    wait(first)
    total = local[...] + jnp.sum(heads[...].astype(F32), axis=0)
    heads[0] = total.astype(BF16)
    mover.put(heads.at[0], out_ref.at[:HUB])
    mover.drain()


def finish(grad, local, weights, mine, side, heads):
    width = grad.shape[1]
    return pl.pallas_call(
        finish_kernel,
        in_specs=[ANY] * (5 + len(heads)),
        out_specs=[ANY] * 3,
        out_shape=[
            jax.ShapeDtypeStruct(grad.shape, BF16),
            jax.ShapeDtypeStruct((width, width), F32),
            jax.ShapeDtypeStruct((width, width), F32),
        ],
        scratch_shapes=[
            pltpu.VMEM((HUB, width), F32),
            pltpu.VMEM((2 * width, width), BF16),
            pltpu.VMEM((2 * width, width), F32),
            pltpu.VMEM((len(heads) + 2, HUB, width), BF16),
            pltpu.SemaphoreType.DMA((len(heads) + 7,)),
        ],
        input_output_aliases={0: 0},
        compiler_params=pltpu.CompilerParams(vmem_limit_bytes=8 * 2**20),
        cost_estimate=pl.CostEstimate(flops=weights.size, bytes_accessed=8 * weights.size, transcendentals=0),
        name="finish",
    )(grad, local, weights, mine, side, *heads)


def trade(value, axis, k):
    return lax.ppermute(value, axis, [(r, r ^ k) for r in range(lax.axis_size(axis))])


def on_device(
    features,
    cotangent,
    self_weight,
    neighbor_weight,
    tile_values,
    tile_index,
    hub_adjacency,
    hub_owner,
    send_rows,
    cut_adjacency,
    degrees,
):
    count, width = features.shape
    groups = lax.axis_size("grp")
    row_count = lax.axis_size("row")
    everyone = ("grp", "row")
    values = tile_values[0]
    index = tile_index.transpose(0, 2, 1)
    degrees = degrees.reshape(count // TILE, TILE)

    head = features[:HUB]
    evens = [head] + [trade(head, "row", k) for k in range(2, row_count, 2)]
    rows, evens[1] = lax.optimization_barrier((send_rows, evens[1]))
    odds, *pieces = pick_rows(rows, features)
    pieces = [pieces[0]] + [trade(pieces[k], "grp", 2 * k) for k in range(1, groups // 2)]
    odds = trade(odds, "grp", 1)
    odds, pieces = lax.optimization_barrier((odds, pieces))
    heads = [x for even in evens for x in (even, trade(even, "row", 1))][1:]
    passed = [odds] + [trade(odds, "grp", 2 * k) for k in range(1, groups // 2)]
    hidden, grad, aggregate, weights, odds, evens, pieces = block(
        index, hub_owner, degrees, self_weight, neighbor_weight, features, values,
        hub_adjacency, cut_adjacency, cotangent, heads, pieces, passed,
    )
    odds = trade(odds, "row", 1)
    parts = weights.reshape(groups * row_count, -1, width)
    parts = lax.all_to_all(parts, everyone, split_axis=0, concat_axis=0, tiled=True)
    heads = [
        trade((even.astype(F32) + odds[j + 1].astype(F32)).astype(BF16), "row", 2 * j + 2)
        for j, even in enumerate(evens[1:])
    ]
    pieces = [pieces[0]] + [trade(pieces[k], "grp", k) for k in range(1, groups)]
    parts, pieces = lax.optimization_barrier((parts, pieces))
    sums = jnp.sum(parts.astype(F32), axis=0).astype(BF16)
    sums = jnp.broadcast_to(sums[None], parts.shape)
    sums = lax.all_to_all(sums, everyone, split_axis=0, concat_axis=0, tiled=True)
    grad_features, head = local_backward(
        index, self_weight, send_rows, values, aggregate, grad, pieces
    )
    grad_features, grad_self, grad_neighbor = finish(
        grad_features, head, sums.reshape(2 * width, width), evens[0], odds, heads
    )
    return hidden, grad_features, grad_self, grad_neighbor


def solution(mesh):
    nodes = P(("grp", "row"), None)
    in_specs = (
        nodes,
        nodes,
        P(),
        P(),
        P(("grp", "row"), None, None, None),
        P(("grp", "row"), None, None),
        nodes,
        P("grp", None),
        P(("grp", "row"), None, None),
        nodes,
        P(("grp", "row")),
    )
    out_specs = (nodes, nodes, P(), P())
    return jax.shard_map(
        on_device, mesh=mesh, in_specs=in_specs, out_specs=out_specs, check_vma=False
    )
```
